512 devices in a mesh: dp: 64 (over y, z_hi, x), fsdp: 2 (over core), tensor: 4 (over z_lo).
Axes of the slice: x: 4, y: 4, z: 16 (z_hi: 4, z_lo: 4; z = z_hi * 4 + z_lo), core: 2. Of those that a mesh axis runs over, the one named last changes fastest.
Arguments:
- x_heads: bfloat16 [32768, 2560], P(('dp', 'fsdp'), 'tensor'), may hold values from -24 to 24
- proj_weight: bfloat16 [2560, 2560], P('tensor', 'fsdp'), may hold values from -0.125 to 0.125
- out_grad: bfloat16 [32768, 2560], P(('dp', 'fsdp', 'tensor')), may hold values from -6 to 6
- proj_basis: bfloat16 [2560, 512], P('dp'), may hold values from -0.125 to 0.125
- first_moment: float32 [4, 640, 512], P('tensor', 'dp'), as said below
- second_moment: float32 [4, 640, 512], P('tensor', 'dp'), may hold values from 32 to 328, as said below
Outputs:
- mixed_out: bfloat16 [32768, 2560], P(('dp', 'fsdp', 'tensor'))
- head_grad: bfloat16 [32768, 2560], P(('dp', 'fsdp'), 'tensor')
- update: bfloat16 [2560, 2560], P('tensor', 'fsdp')
The draws below stay inside these ranges and needn't reach their ends.
Inputs may be any that keep to these rules, and one draw needn't show every extreme that they name: `first_moment`: entries within plus or minus 0.4 times the square root of 32768. `second_moment`: positive, between 32768 / 1000 and 32768 / 100.
All inputs are finite; a program needn't handle non-finite values.
Results may differ from the reference program's by a relative error of at most 0.0056.
Values may be sent and summed in bfloat16 or wider, within the bound.
No kernel may reach another device: no remote copies, remote signals or barrier semaphores. Data moves between devices by JAX's collectives and lax.ppermute only.
A program may use at most 64 MiB of HBM per device.

```python
import math
import jax
import jax.numpy as jnp
from jax import lax

DW = 2560
RANK = 512
ADAM_STEP = 10
HD = 2560
HD_DEV = 640
TOKENS = 32768


def draw_first_moment(key, part):
    key = jax.random.fold_in(key, 11)
    values = jax.random.truncated_normal(key, -4.0, 4.0, (HD // HD_DEV, HD_DEV, RANK), jnp.float32)
    return 0.1 * math.sqrt(TOKENS) * values


def draw_second_moment(key, part):
    key = jax.random.fold_in(key, 12)
    logs = jax.random.uniform(key, (HD // HD_DEV, HD_DEV, RANK), jnp.float32, math.log(0.0011), math.log(0.0099))
    return TOKENS * jnp.exp(logs)


def spiked(values, rng, source, target, blocks, factor):
    def block_of(dim):
        return (jnp.arange(values.shape[dim]) // (values.shape[dim] // blocks)).reshape((-1,) + (1,) * (values.ndim - 1 - dim))

    near = jax.random.permutation(rng, blocks)[block_of(target)]
    second = (block_of(target) + blocks // 2) % blocks
    return jnp.where((block_of(source) == near) | (block_of(source) == second), factor * values, values)


def level_of(stream_key, dims, split, smallest, largest):
    def one(position, blocks):
        steps = jax.random.uniform(jax.random.fold_in(jax.random.fold_in(stream_key, 6), position), (blocks,), jnp.float32, smallest / len(split), largest / len(split))
        return jnp.repeat(jnp.exp(steps), dims[position] // blocks).reshape((-1,) + (1,) * (len(dims) - position - 1))

    factor_of = one(*split[0])
    for cut in split[1:]:
        factor_of = factor_of * one(*cut)
    return factor_of


def gaussian(own_key, extent, width, reach, split=(), held_as=jnp.bfloat16):
    entries = jax.random.normal(own_key, extent, jnp.float32) * width
    if len(split) > 0:
        entries = level_of(own_key, extent, split, -0.22, 0.18) * entries
    return jnp.clip(entries, min=-reach, max=reach).astype(held_as)


def bell_draw_with(stream_key, extent, scale, most, split, heavy, held_as=jnp.bfloat16):
    result = scale * jax.random.normal(stream_key, extent, jnp.float32)
    if split:
        result = result * level_of(stream_key, extent, split, -0.22, 0.18)
    return jnp.clip(spiked(result, jax.random.fold_in(stream_key, 3), *heavy), -most, most).astype(held_as)


def setup_inputs(seed: int = 0) -> dict:
    seeds = jax.random.split(jax.random.key(seed), 7)
    return {
        "x_heads": bell_draw_with(seeds[0], (TOKENS, HD), 1.0, 24.0, ((0, 128), (1, 4)), (0, 1, 128, 5.5)),
        "proj_weight": gaussian(seeds[1], (HD, DW), HD ** -0.5, 0.125, ((0, 4), (1, 2))),
        "out_grad": gaussian(seeds[2], (TOKENS, DW), 1.0, 6.0, ((0, 512),)),
        "proj_basis": gaussian(seeds[3], (DW, RANK), DW ** -0.5, 0.125, ((0, 64),)),
        "first_moment": draw_first_moment(jax.random.fold_in(seeds[6], 71), 0),
        "second_moment": draw_second_moment(jax.random.fold_in(seeds[6], 71), 0),
    }


def reference(x_heads, proj_weight, out_grad, proj_basis, first_moment, second_moment):
    mixed_out = jnp.dot(x_heads, proj_weight, preferred_element_type=jnp.float32).astype(jnp.bfloat16)
    head_grad = lax.dot_general(out_grad, proj_weight, (((1,), (1,)), ((), ())), preferred_element_type=jnp.float32).astype(jnp.bfloat16)
    reduced = jnp.dot(out_grad, proj_basis, preferred_element_type=jnp.float32).astype(jnp.bfloat16)
    low_grad = lax.dot_general(x_heads, reduced, (((0,), (0,)), ((), ())), preferred_element_type=jnp.float32)
    moment_one = first_moment.reshape(HD, RANK)
    moment_two = second_moment.reshape(HD, RANK)
    m_new = 0.9 * moment_one + 0.1 * low_grad
    v_new = 0.999 * moment_two + 0.001 * low_grad * low_grad
    corr_one = 1.0 - 0.9 ** ADAM_STEP
    corr_two = 1.0 - 0.999 ** ADAM_STEP
    direction = (m_new / corr_one / (jnp.sqrt(v_new / corr_two) + 1e-08)).astype(jnp.bfloat16)
    update = lax.dot_general(direction, proj_basis, (((1,), (1,)), ((), ())), preferred_element_type=jnp.float32).astype(jnp.bfloat16)
    return (mixed_out, head_grad, update)
```

```python
import jax
import jax.numpy as jnp
from jax import lax
from jax.sharding import Mesh, PartitionSpec as P

ADAM_STEP = 10
BF16 = jnp.bfloat16
F32 = jnp.float32
AXES = ("y", "zh", "x", "core", "zl")
SIZES = (4, 4, 4, 2, 4)
CORE_SWAP = [(0, 1), (1, 0)]
PAIR = [(0, 1), (1, 0), (2, 3), (3, 2)]
MIRROR = [(0, 3), (3, 0), (1, 2), (2, 1)]
TURN = [(a * 4 + b, b * 4 + a) for a in range(4) for b in range(4)]


def spread(values, axes, count):
    copies = jnp.broadcast_to(values[None], (count,) + values.shape)
    return lax.all_to_all(copies, axes, 0, 0, tiled=True)


def gather_zh(values, beside):
    zh = lax.axis_index("zh")
    got = lax.ppermute(values, "zh", PAIR)
    odd = zh % 2 == 1
    pair = jnp.concatenate([jnp.where(odd, got, values), jnp.where(odd, values, got)], 0)
    got = lax.ppermute(pair, "zh", MIRROR)
    got, beside = lax.optimization_barrier((got, beside))
    high = zh >= 2
    both = jnp.stack([jnp.where(high, got, pair), jnp.where(high, pair, got)])
    return both.reshape(4, *values.shape), beside


def sum_zh(values, beside):
    sent = values.astype(BF16)
    got = lax.ppermute(sent, "zh", PAIR)
    got, beside = lax.optimization_barrier((got, beside))
    sent = (sent.astype(F32) + got.astype(F32)).astype(BF16)
    got = lax.ppermute(sent, "zh", MIRROR)
    return sent.astype(F32) + got.astype(F32), beside


def shards(x_heads, proj_weight, out_grad, proj_basis, first_moment, second_moment):
    core = lax.axis_index("core")
    zl = lax.axis_index("zl")
    half = proj_weight.shape[1]

    grad_block = lax.all_gather(out_grad, "zl", axis=0, tiled=True)

    def own_columns(moment):
        cols = lax.dynamic_slice_in_dim(moment[0], core * 256, 256, 1).astype(BF16)
        return [cols[:, :128], cols[:, 128:]]

    moments = jnp.concatenate(own_columns(first_moment) + own_columns(second_moment), 0)
    moments = lax.ppermute(moments, ("zh", "x"), TURN)

    weight_other = lax.ppermute(proj_weight, "core", CORE_SWAP)
    weight_full = jnp.zeros((proj_weight.shape[0], 2 * half), BF16)
    weight_full = lax.dynamic_update_slice(weight_full, proj_weight, (0, core * half))
    weight_full = lax.dynamic_update_slice(weight_full, weight_other, (0, (1 - core) * half))

    mixed_part = jnp.dot(x_heads, weight_full, preferred_element_type=F32).astype(BF16)

    basis_own = lax.dynamic_slice_in_dim(proj_basis, zl * 128, 128, 1)
    by_zh, mixed_part = gather_zh(jnp.concatenate([basis_own, moments], 0), mixed_part)
    basis_zh = by_zh[:, :40]
    moment_zh = by_zh[:, 40:].reshape(4, 2, 2, 10, 128)
    m_old = moment_zh[:, 0].transpose(0, 2, 1, 3).reshape(40, 256).astype(F32)
    v_old = moment_zh[:, 1].transpose(0, 2, 1, 3).reshape(40, 256).astype(F32)
    by_yx = spread(basis_zh.reshape(160, 128), ("y", "x"), 16)
    basis_cols = (
        by_yx.reshape(4, 4, 4, 40, 128).transpose(0, 2, 1, 3, 4).reshape(2560, 128)
    )

    mixed_out = lax.psum_scatter(mixed_part, "zl", scatter_dimension=0, tiled=True)

    basis_half = lax.all_gather(
        lax.dynamic_slice_in_dim(basis_cols, core * half, half, 0), "zl", axis=0, tiled=False
    )

    reduced_part = jnp.dot(grad_block, basis_cols, preferred_element_type=F32).astype(BF16)
    reduced = spread(reduced_part, "zl", 4)

    def low_columns(which):
        cols = lax.dynamic_slice_in_dim(reduced, 2 * which, 2, 0)
        cols = cols.transpose(1, 0, 2).reshape(256, 256)
        return lax.dot_general(x_heads, cols, (((0,), (0,)), ((), ())), preferred_element_type=F32)

    low_sent = low_columns(1 - core).astype(BF16)
    low_got = lax.ppermute(low_sent, "core", CORE_SWAP)
    low_chip = (low_columns(core) + low_got.astype(F32)).astype(BF16)

    low_yx = lax.all_to_all(low_chip.reshape(16, 40, 256), ("y", "x"), 0, 0, tiled=True)
    head_rows = lax.dot_general(
        grad_block, weight_full, (((1,), (1,)), ((), ())), preferred_element_type=F32
    ).astype(BF16)
    low, head_rows = sum_zh(jnp.sum(low_yx.astype(F32), 0), head_rows)

    m_new = 0.9 * m_old + 0.1 * low
    v_new = 0.999 * v_old + 0.001 * low * low
    corr_one = 1.0 - 0.9**ADAM_STEP
    corr_two = 1.0 - 0.999**ADAM_STEP
    direction = (m_new / corr_one / (jnp.sqrt(v_new / corr_two) + 1e-08)).astype(BF16)

    rows = spread(direction, ("y", "x"), 16).reshape(640, 256)
    rows_other = lax.ppermute(rows, "core", CORE_SWAP)

    def half_update(columns, which):
        cols = lax.dynamic_slice_in_dim(basis_half, 2 * which, 2, 0)
        cols = cols.transpose(1, 0, 2).reshape(half, 256)
        return lax.dot_general(columns, cols, (((1,), (1,)), ((), ())), preferred_element_type=F32)

    update = (half_update(rows, core) + half_update(rows_other, 1 - core)).astype(BF16)
    return (mixed_out, head_rows, update)


def solution(mesh):
    fine = Mesh(mesh.devices.reshape(SIZES), AXES)
    dp = ("y", "zh", "x")
    return jax.shard_map(
        shards,
        mesh=fine,
        in_specs=(
            P(dp + ("core",), "zl"),
            P("zl", "core"),
            P(dp + ("core", "zl"), None),
            P(dp, None),
            P("zl", dp, None),
            P("zl", dp, None),
        ),
        out_specs=(
            P(dp + ("core", "zl"), None),
            P(dp + ("core",), "zl"),
            P("zl", "core"),
        ),
        check_vma=False,
    )
```

```python
import jax
import jax.numpy as jnp
from jax import lax
from jax.experimental import pallas as pl
from jax.experimental.pallas import tpu as pltpu
from jax.sharding import Mesh, PartitionSpec as P

ADAM_STEP = 10
BF16 = jnp.bfloat16
F32 = jnp.float32
AXES = ("y", "zh", "x", "core", "zl")
SIZES = (4, 4, 4, 2, 4)
CORE_SWAP = [(0, 1), (1, 0)]
PAIR = [(0, 1), (1, 0), (2, 3), (3, 2)]
MIRROR = [(0, 3), (3, 0), (1, 2), (2, 1)]
TURN = [(a * 4 + b, b * 4 + a) for a in range(4) for b in range(4)]


def spread(values, axes, count):
    copies = jnp.broadcast_to(values[None], (count,) + values.shape)
    return lax.all_to_all(copies, axes, 0, 0, tiled=True)


def gather_zh(values):
    zh = lax.axis_index("zh")
    got = lax.ppermute(values, "zh", PAIR)
    odd = zh % 2 == 1
    pair = jnp.concatenate([jnp.where(odd, got, values), jnp.where(odd, values, got)], 0)
    got = lax.ppermute(pair, "zh", MIRROR)
    high = zh >= 2
    both = jnp.stack([jnp.where(high, got, pair), jnp.where(high, pair, got)])
    return both.reshape(4, *values.shape)


def sum_zh(values):
    for partners in (PAIR, MIRROR):
        sent = values.astype(BF16)
        values = sent.astype(F32) + lax.ppermute(sent, "zh", partners).astype(F32)
    return values


VMEM = pl.BlockSpec(memory_space=pltpu.VMEM)
SMEM = pl.BlockSpec(memory_space=pltpu.SMEM)
ROOM = pltpu.CompilerParams(vmem_limit_bytes=40 * 2**20)


def cost(flops, moved):
    return pl.CostEstimate(flops=flops, bytes_accessed=moved, transcendentals=0)


def columns_of(which, half):
    return pl.ds(pl.multiple_of(which * half, 128), half)


def mixed_kernel(core_ref, x_ref, own_ref, other_ref, out_ref):
    core = core_ref[0]
    half = own_ref.shape[1]
    for which, weight in ((core, own_ref), (1 - core, other_ref)):
        part = jnp.dot(x_ref[...], weight[...], preferred_element_type=F32)
        out_ref[:, columns_of(which, half)] = part.astype(BF16)


def mixed_matmul(core, x_heads, own, other):
    return pl.pallas_call(
        mixed_kernel,
        out_shape=jax.ShapeDtypeStruct((256, 2560), BF16),
        in_specs=[SMEM, VMEM, VMEM, VMEM],
        out_specs=VMEM,
        compiler_params=ROOM,
        cost_estimate=cost(2 * 256 * 640 * 2560, 5_000_000),
    )(core, x_heads, own, other)


def head_kernel(core_ref, grad_ref, own_ref, other_ref, out_ref):
    core = core_ref[0]
    half = own_ref.shape[1]
    total = None
    for which, weight in ((core, own_ref), (1 - core, other_ref)):
        part = lax.dot_general(
            grad_ref[:, columns_of(which, half)],
            weight[...],
            (((1,), (1,)), ((), ())),
            preferred_element_type=F32,
        )
        total = part if total is None else total + part
    out_ref[...] = total.astype(BF16)


def head_matmul(core, grads, own, other):
    return pl.pallas_call(
        head_kernel,
        out_shape=jax.ShapeDtypeStruct((256, 640), BF16),
        in_specs=[SMEM, VMEM, VMEM, VMEM],
        out_specs=VMEM,
        compiler_params=ROOM,
        cost_estimate=cost(2 * 256 * 640 * 2560, 5_000_000),
    )(core, grads, own, other)


def low_kernel(basis_ref, x_ref, grad_ref, *refs):
    out_ref = refs[-1]
    reduced = jnp.dot(grad_ref[...], basis_ref[...], preferred_element_type=F32).astype(BF16)
    low = lax.dot_general(
        x_ref[...], reduced, (((0,), (0,)), ((), ())), preferred_element_type=F32
    )
    if len(refs) == 2:
        low = refs[0][...] + low
    out_ref[...] = low.astype(out_ref.dtype)


def low_matmul(basis, rows, grads, *before):
    return pl.pallas_call(
        low_kernel,
        out_shape=jax.ShapeDtypeStruct((640, 256), BF16 if before else F32),
        in_specs=[VMEM] * (3 + len(before)),
        out_specs=VMEM,
        compiler_params=ROOM,
        cost_estimate=cost(2 * 256 * 256 * (2560 + 640), 3_500_000),
    )(basis, rows, grads, *before)


def shards(x_heads, proj_weight, out_grad, proj_basis, first_moment, second_moment):
    core = lax.axis_index("core")
    half = proj_weight.shape[1]

    scalar = core.reshape(1).astype(jnp.int32)

    grad_block = lax.all_gather(out_grad, "zl", axis=0, tiled=True)

    def own_columns(values):
        return lax.dynamic_slice_in_dim(values, core * 256, 256, 1)

    moments = jnp.concatenate([own_columns(first_moment[0]), own_columns(second_moment[0])], 0)
    moments = lax.ppermute(moments.astype(BF16), ("zh", "x"), TURN)

    weight_other = lax.ppermute(proj_weight, "core", CORE_SWAP)
    x_other = lax.ppermute(x_heads, "core", CORE_SWAP)
    by_zh = gather_zh(jnp.concatenate([own_columns(proj_basis), moments], 0))
    by_zh, weight_other = lax.optimization_barrier((by_zh, weight_other))
    m_old = by_zh[:, 40:50].reshape(40, 256)
    v_old = by_zh[:, 50:].reshape(40, 256)
    by_yx = spread(by_zh[:, :40].reshape(160, 256), ("y", "x"), 16)
    mixed_part = mixed_matmul(scalar, x_heads, proj_weight, weight_other)
    by_yx, mixed_part, grad_block, x_other = lax.optimization_barrier(
        (by_yx, mixed_part, grad_block, x_other)
    )
    grad_other = lax.ppermute(grad_block, "core", CORE_SWAP)
    basis_cols = by_yx.reshape(4, 4, 4, 40, 256).transpose(0, 2, 1, 3, 4).reshape(2560, 256)

    mixed_out = lax.psum_scatter(mixed_part, "zl", scatter_dimension=0, tiled=True)

    low_own = low_matmul(basis_cols, x_heads, grad_block)
    low_chip = low_matmul(basis_cols, x_other, grad_other, low_own)

    low_yx = lax.all_to_all(low_chip.reshape(16, 40, 256), ("y", "x"), 0, 0, tiled=True)
    basis_cols, low_chip = lax.optimization_barrier((basis_cols, low_chip))
    basis_own = lax.dynamic_slice_in_dim(basis_cols, core * half, half, 0)
    basis_other = lax.ppermute(
        lax.dynamic_slice_in_dim(basis_cols, (1 - core) * half, half, 0), "core", CORE_SWAP
    )
    low_yx, basis_other = lax.optimization_barrier((low_yx, basis_other))
    low = sum_zh(jnp.sum(low_yx.astype(F32), 0))

    m_new = 0.9 * m_old.astype(F32) + 0.1 * low
    v_new = 0.999 * v_old.astype(F32) + 0.001 * low * low
    corr_one = 1.0 - 0.9**ADAM_STEP
    corr_two = 1.0 - 0.999**ADAM_STEP
    direction = (m_new / corr_one / (jnp.sqrt(v_new / corr_two) + 1e-08)).astype(BF16)

    rows = spread(direction, ("y", "x"), 16).reshape(640, 256)
    head_rows = head_matmul(scalar, grad_block, proj_weight, weight_other)
    rows, head_rows, mixed_out = lax.optimization_barrier((rows, head_rows, mixed_out))
    rows_other = lax.ppermute(rows, "core", CORE_SWAP)

    def half_update(columns, basis):
        return lax.dot_general(columns, basis, (((1,), (1,)), ((), ())), preferred_element_type=F32)

    update = (half_update(rows, basis_own) + half_update(rows_other, basis_other)).astype(BF16)
    return (mixed_out, head_rows, update)


def solution(mesh):
    fine = Mesh(mesh.devices.reshape(SIZES), AXES)
    dp = ("y", "zh", "x")
    return jax.shard_map(
        shards,
        mesh=fine,
        in_specs=(
            P(dp + ("core",), "zl"),
            P("zl", "core"),
            P(dp + ("core", "zl"), None),
            P(dp, None),
            P("zl", dp, None),
            P("zl", dp, None),
        ),
        out_specs=(
            P(dp + ("core", "zl"), None),
            P(dp + ("core",), "zl"),
            P("zl", "core"),
        ),
        check_vma=False,
    )
```

```python
import jax
import jax.numpy as jnp
from jax import lax
from jax.experimental import pallas as pl
from jax.experimental.pallas import tpu as pltpu
from jax.sharding import Mesh, PartitionSpec as P

ADAM_STEP = 10
BF16 = jnp.bfloat16
F32 = jnp.float32
AXES = ("y", "zh", "x", "core", "zl")
SIZES = (4, 4, 4, 2, 4)
CORE_SWAP = [(0, 1), (1, 0)]
PAIR = [(0, 1), (1, 0), (2, 3), (3, 2)]
MIRROR = [(0, 3), (3, 0), (1, 2), (2, 1)]
TURN = [(a * 4 + b, b * 4 + a) for a in range(4) for b in range(4)]


def spread(values, axes, count):
    copies = jnp.broadcast_to(values[None], (count,) + values.shape)
    return lax.all_to_all(copies, axes, 0, 0, tiled=True)


def gather_zh(values):
    zh = lax.axis_index("zh")
    got = lax.ppermute(values, "zh", PAIR)
    odd = zh % 2 == 1
    pair = jnp.concatenate([jnp.where(odd, got, values), jnp.where(odd, values, got)], 0)
    got = lax.ppermute(pair, "zh", MIRROR)
    high = zh >= 2
    both = jnp.stack([jnp.where(high, got, pair), jnp.where(high, pair, got)])
    return both.reshape(4, *values.shape)


def sum_zh(values):
    for partners in (PAIR, MIRROR):
        sent = values.astype(BF16)
        values = sent.astype(F32) + lax.ppermute(sent, "zh", partners).astype(F32)
    return values


VMEM = pl.BlockSpec(memory_space=pltpu.VMEM)
SMEM = pl.BlockSpec(memory_space=pltpu.SMEM)
ROOM = pltpu.CompilerParams(vmem_limit_bytes=40 * 2**20)


def cost(flops, moved):
    return pl.CostEstimate(flops=flops, bytes_accessed=moved, transcendentals=0)


def columns_of(which, half):
    return pl.ds(pl.multiple_of(which * half, 128), half)


def mixed_kernel(core_ref, x_ref, own_ref, other_ref, out_ref):
    core = core_ref[0]
    half = own_ref.shape[1]
    for which, weight in ((core, own_ref), (1 - core, other_ref)):
        part = jnp.dot(x_ref[...], weight[...], preferred_element_type=F32)
        out_ref[:, columns_of(which, half)] = part.astype(BF16)


def mixed_matmul(core, x_heads, own, other):
    return pl.pallas_call(
        mixed_kernel,
        out_shape=jax.ShapeDtypeStruct((256, 2560), BF16),
        in_specs=[SMEM, VMEM, VMEM, VMEM],
        out_specs=VMEM,
        compiler_params=ROOM,
        cost_estimate=cost(2 * 256 * 640 * 2560, 5_000_000),
    )(core, x_heads, own, other)


def head_kernel(core_ref, grad_ref, own_ref, other_ref, out_ref):
    core = core_ref[0]
    half = own_ref.shape[1]
    total = None
    for which, weight in ((core, own_ref), (1 - core, other_ref)):
        part = lax.dot_general(
            grad_ref[:, columns_of(which, half)],
            weight[...],
            (((1,), (1,)), ((), ())),
            preferred_element_type=F32,
        )
        total = part if total is None else total + part
    out_ref[...] = total.astype(BF16)


def head_matmul(core, grads, own, other):
    return pl.pallas_call(
        head_kernel,
        out_shape=jax.ShapeDtypeStruct((256, 640), BF16),
        in_specs=[SMEM, VMEM, VMEM, VMEM],
        out_specs=VMEM,
        compiler_params=ROOM,
        cost_estimate=cost(2 * 256 * 640 * 2560, 5_000_000),
    )(core, grads, own, other)


def reduced_kernel(basis_ref, own_ref, other_ref, out_ref):
    for which, grads in ((0, own_ref), (1, other_ref)):
        part = jnp.dot(grads[...], basis_ref[...], preferred_element_type=F32).astype(BF16)
        for target in range(out_ref.shape[0]):
            out_ref[target, which] = part


def reduced_matmul(basis, grads, grads_other):
    return pl.pallas_call(
        reduced_kernel,
        out_shape=jax.ShapeDtypeStruct((4, 2, 64, 256), BF16),
        in_specs=[VMEM] * 3,
        out_specs=VMEM,
        compiler_params=ROOM,
        cost_estimate=cost(2 * 128 * 256 * 2560, 2_500_000),
    )(basis, grads, grads_other)


def low_kernel(reduced_ref, own_ref, other_ref, out_ref):
    total = None
    for which, rows in ((0, own_ref), (1, other_ref)):
        reduced = reduced_ref[:, which].reshape(256, 256)
        part = lax.dot_general(
            rows[...], reduced, (((0,), (0,)), ((), ())), preferred_element_type=F32
        )
        total = part if total is None else total + part
    out_ref[...] = total.astype(BF16)


def low_matmul(reduced, rows, rows_other):
    return pl.pallas_call(
        low_kernel,
        out_shape=jax.ShapeDtypeStruct((640, 256), BF16),
        in_specs=[VMEM] * 3,
        out_specs=VMEM,
        compiler_params=ROOM,
        cost_estimate=cost(2 * 512 * 256 * 640, 1_500_000),
    )(reduced, rows, rows_other)


def shards(x_heads, proj_weight, out_grad, proj_basis, first_moment, second_moment):
    core = lax.axis_index("core")
    half = proj_weight.shape[1]
    scalar = core.reshape(1).astype(jnp.int32)

    def own_columns(values):
        return lax.dynamic_slice_in_dim(values, core * 256, 256, 1)

    grad_block = lax.all_gather(out_grad, "zl", axis=0, tiled=True)
    weight_other = lax.ppermute(proj_weight, "core", CORE_SWAP)
    grad_other = lax.ppermute(out_grad, "core", CORE_SWAP)
    x_other = lax.ppermute(x_heads, "core", CORE_SWAP)

    by_zh = gather_zh(own_columns(proj_basis)).reshape(160, 256)
    moments = [own_columns(first_moment[0]), own_columns(second_moment[0])]
    by_yx = spread(jnp.concatenate([by_zh] + [m.astype(BF16) for m in moments], 0), ("y", "x"), 16)

    mixed_part = mixed_matmul(scalar, x_heads, proj_weight, weight_other)
    by_yx, mixed_part, grad_other, x_other = lax.optimization_barrier(
        (by_yx, mixed_part, grad_other, x_other)
    )
    moments = lax.dynamic_slice_in_dim(by_yx[:, 160:], 4 * lax.axis_index("y"), 4, 0)
    by_yx = by_yx[:, :160]
    basis_cols = by_yx.reshape(4, 4, 4, 40, 256).transpose(0, 2, 1, 3, 4).reshape(2560, 256)

    mixed_out = lax.psum_scatter(mixed_part, "zl", scatter_dimension=0, tiled=True)

    reduced = reduced_matmul(basis_cols, out_grad, grad_other)
    reduced = lax.all_to_all(reduced, "zl", 0, 0, tiled=True)
    basis_own = lax.dynamic_slice_in_dim(basis_cols, core * half, half, 0)
    basis_other = lax.ppermute(
        lax.dynamic_slice_in_dim(basis_cols, (1 - core) * half, half, 0), "core", CORE_SWAP
    )
    reduced, basis_other = lax.optimization_barrier((reduced, basis_other))

    low_chip = low_matmul(reduced, x_heads, x_other)

    low_yx = lax.all_to_all(low_chip.reshape(16, 40, 256), ("y", "x"), 0, 0, tiled=True)
    moments, low_chip = lax.optimization_barrier((moments, low_chip))
    moments = lax.ppermute(moments, ("zh", "x"), TURN)
    low_yx, moments = lax.optimization_barrier((low_yx, moments))
    m_old = moments[:, :10].reshape(40, 256)
    v_old = moments[:, 10:].reshape(40, 256)
    low = sum_zh(jnp.sum(low_yx.astype(F32), 0))

    m_new = 0.9 * m_old.astype(F32) + 0.1 * low
    v_new = 0.999 * v_old.astype(F32) + 0.001 * low * low
    corr_one = 1.0 - 0.9**ADAM_STEP
    corr_two = 1.0 - 0.999**ADAM_STEP
    direction = (m_new / corr_one / (jnp.sqrt(v_new / corr_two) + 1e-08)).astype(BF16)

    rows = spread(direction, ("y", "x"), 16).reshape(640, 256)
    head_rows = head_matmul(scalar, grad_block, proj_weight, weight_other)
    rows, head_rows, mixed_out = lax.optimization_barrier((rows, head_rows, mixed_out))
    rows_other = lax.ppermute(rows, "core", CORE_SWAP)

    def half_update(columns, basis):
        return lax.dot_general(columns, basis, (((1,), (1,)), ((), ())), preferred_element_type=F32)

    update = (half_update(rows, basis_own) + half_update(rows_other, basis_other)).astype(BF16)
    return (mixed_out, head_rows, update)


def solution(mesh):
    fine = Mesh(mesh.devices.reshape(SIZES), AXES)
    dp = ("y", "zh", "x")
    return jax.shard_map(
        shards,
        mesh=fine,
        in_specs=(
            P(dp + ("core",), "zl"),
            P("zl", "core"),
            P(dp + ("core", "zl"), None),
            P(dp, None),
            P("zl", dp, None),
            P("zl", dp, None),
        ),
        out_specs=(
            P(dp + ("core", "zl"), None),
            P(dp + ("core",), "zl"),
            P("zl", "core"),
        ),
        check_vma=False,
    )
```

```python
import jax
import jax.numpy as jnp
import numpy as np
from jax import lax
from jax.experimental import pallas as pl
from jax.experimental.pallas import tpu as pltpu
from jax.sharding import Mesh, PartitionSpec as P

ADAM_STEP = 10
BF16 = jnp.bfloat16
F32 = jnp.float32
AXES = ("y", "zh", "x", "core", "zl")
SIZES = (4, 4, 4, 2, 4)
CORE_SWAP = [(0, 1), (1, 0)]
PAIR = [(0, 1), (1, 0), (2, 3), (3, 2)]
MIRROR = [(0, 3), (3, 0), (1, 2), (2, 1)]
ORDER = np.eye(640, dtype=np.float32).reshape(640, 4, 4, 4, 10).transpose(0, 1, 3, 2, 4).reshape(640, 640)


def spread(values, axes, count):
    copies = jnp.broadcast_to(values[None], (count,) + values.shape)
    return lax.all_to_all(copies, axes, 0, 0, tiled=True)


def gather_zh(values):
    zh = lax.axis_index("zh")
    got = lax.ppermute(values, "zh", PAIR)
    odd = zh % 2 == 1
    pair = jnp.concatenate([jnp.where(odd, got, values), jnp.where(odd, values, got)], 0)
    got = lax.ppermute(pair, "zh", MIRROR)
    high = zh >= 2
    both = jnp.stack([jnp.where(high, got, pair), jnp.where(high, pair, got)])
    return both.reshape(4, *values.shape)


def sum_zh(values):
    for partners in (PAIR, MIRROR):
        sent = values.astype(BF16)
        values = sent.astype(F32) + lax.ppermute(sent, "zh", partners).astype(F32)
    return values


VMEM = pl.BlockSpec(memory_space=pltpu.VMEM)
SMEM = pl.BlockSpec(memory_space=pltpu.SMEM)
ROOM = pltpu.CompilerParams(vmem_limit_bytes=40 * 2**20)


def cost(flops, moved):
    return pl.CostEstimate(flops=flops, bytes_accessed=moved, transcendentals=0)


def columns_of(which, half):
    return pl.ds(pl.multiple_of(which * half, 128), half)


def mixed_kernel(core_ref, x_ref, own_ref, other_ref, out_ref):
    core = core_ref[0]
    half = own_ref.shape[1]
    for which, weight in ((core, own_ref), (1 - core, other_ref)):
        part = jnp.dot(x_ref[...], weight[...], preferred_element_type=F32)
        out_ref[:, columns_of(which, half)] = part.astype(BF16)


def mixed_matmul(core, x_heads, own, other):
    return pl.pallas_call(
        mixed_kernel,
        out_shape=jax.ShapeDtypeStruct((256, 2560), BF16),
        in_specs=[SMEM, VMEM, VMEM, VMEM],
        out_specs=VMEM,
        compiler_params=ROOM,
        cost_estimate=cost(2 * 256 * 640 * 2560, 5_000_000),
    )(core, x_heads, own, other)


def head_kernel(core_ref, grad_ref, own_ref, other_ref, out_ref):
    core = core_ref[0]
    half = own_ref.shape[1]
    total = None
    for which, weight in ((core, own_ref), (1 - core, other_ref)):
        part = lax.dot_general(
            grad_ref[:, columns_of(which, half)],
            weight[...],
            (((1,), (1,)), ((), ())),
            preferred_element_type=F32,
        )
        total = part if total is None else total + part
    out_ref[...] = total.astype(BF16)


def head_matmul(core, grads, own, other):
    return pl.pallas_call(
        head_kernel,
        out_shape=jax.ShapeDtypeStruct((256, 640), BF16),
        in_specs=[SMEM, VMEM, VMEM, VMEM],
        out_specs=VMEM,
        compiler_params=ROOM,
        cost_estimate=cost(2 * 256 * 640 * 2560, 5_000_000),
    )(core, grads, own, other)


def reduced_kernel(basis_ref, own_ref, other_ref, out_ref):
    for which, grads in ((0, own_ref), (1, other_ref)):
        part = jnp.dot(grads[...], basis_ref[...], preferred_element_type=F32).astype(BF16)
        for target in range(out_ref.shape[0]):
            out_ref[target, which] = part


def reduced_matmul(basis, grads, grads_other):
    return pl.pallas_call(
        reduced_kernel,
        out_shape=jax.ShapeDtypeStruct((4, 2, 64, 256), BF16),
        in_specs=[VMEM] * 3,
        out_specs=VMEM,
        compiler_params=ROOM,
        cost_estimate=cost(2 * 128 * 256 * 2560, 2_500_000),
    )(basis, grads, grads_other)


def low_kernel(reduced_ref, own_ref, other_ref, order_ref, out_ref):
    total = None
    for which, rows in ((0, own_ref), (1, other_ref)):
        reduced = reduced_ref[:, which].reshape(256, 256)
        part = lax.dot_general(
            rows[...], reduced, (((0,), (0,)), ((), ())), preferred_element_type=F32
        )
        total = part if total is None else total + part
    ordered = lax.dot_general(
        order_ref[...], total.astype(BF16), (((0,), (0,)), ((), ())), preferred_element_type=F32
    )
    out_ref[...] = ordered.astype(BF16)


def low_matmul(reduced, rows, rows_other, order):
    return pl.pallas_call(
        low_kernel,
        out_shape=jax.ShapeDtypeStruct((640, 256), BF16),
        in_specs=[VMEM] * 4,
        out_specs=VMEM,
        compiler_params=ROOM,
        cost_estimate=cost(2 * 640 * 256 * (512 + 640), 2_300_000),
    )(reduced, rows, rows_other, order)


def update_kernel(own_ref, other_ref, order_ref, basis_ref, basis_other_ref, out_ref):
    total = None
    for rows, basis in ((own_ref, basis_ref), (other_ref, basis_other_ref)):
        direction = jnp.dot(order_ref[...], rows[...], preferred_element_type=F32).astype(BF16)
        part = lax.dot_general(
            direction, basis[...], (((1,), (1,)), ((), ())), preferred_element_type=F32
        )
        total = part if total is None else total + part
    out_ref[...] = total.astype(BF16)


def update_matmul(rows, rows_other, order, basis, basis_other):
    half = basis.shape[0]
    return pl.pallas_call(
        update_kernel,
        out_shape=jax.ShapeDtypeStruct((640, half), BF16),
        in_specs=[VMEM] * 5,
        out_specs=VMEM,
        compiler_params=ROOM,
        cost_estimate=cost(2 * 640 * 512 * (640 + half), 5_000_000),
    )(rows, rows_other, order, basis, basis_other)


def shards(x_heads, proj_weight, out_grad, proj_basis, first_moment, second_moment):
    core = lax.axis_index("core")
    half = proj_weight.shape[1]
    scalar = core.reshape(1).astype(jnp.int32)

    def own_columns(values):
        return lax.dynamic_slice_in_dim(values, core * 256, 256, 1)

    grad_block = lax.all_gather(out_grad, "zl", axis=0, tiled=True)
    weight_other = lax.ppermute(proj_weight, "core", CORE_SWAP)
    grad_other = lax.ppermute(out_grad, "core", CORE_SWAP)
    x_other = lax.ppermute(x_heads, "core", CORE_SWAP)

    parts = [proj_basis, first_moment[0].astype(BF16), second_moment[0].astype(BF16)]
    by_zh = gather_zh(jnp.concatenate([own_columns(part) for part in parts], 0))
    m_old = by_zh[:, 40:50].reshape(40, 256)
    v_old = by_zh[:, 50:].reshape(40, 256)
    by_yx = spread(by_zh[:, :40].reshape(160, 256), ("y", "x"), 16)

    mixed_part = mixed_matmul(scalar, x_heads, proj_weight, weight_other)
    by_yx, mixed_part, grad_other, x_other, m_old, v_old = lax.optimization_barrier(
        (by_yx, mixed_part, grad_other, x_other, m_old, v_old)
    )
    basis_cols = by_yx.reshape(4, 4, 4, 40, 256).transpose(0, 2, 1, 3, 4).reshape(2560, 256)

    mixed_out = lax.psum_scatter(mixed_part, "zl", scatter_dimension=0, tiled=True)

    reduced = reduced_matmul(basis_cols, out_grad, grad_other)
    reduced = lax.all_to_all(reduced, "zl", 0, 0, tiled=True)
    basis_own = lax.dynamic_slice_in_dim(basis_cols, core * half, half, 0)
    basis_other = lax.ppermute(
        lax.dynamic_slice_in_dim(basis_cols, (1 - core) * half, half, 0), "core", CORE_SWAP
    )
    reduced, basis_other = lax.optimization_barrier((reduced, basis_other))

    order = jnp.asarray(ORDER, BF16)
    low_chip = low_matmul(reduced, x_heads, x_other, order)

    low_yx = lax.all_to_all(low_chip.reshape(16, 40, 256), ("y", "x"), 0, 0, tiled=True)
    low = sum_zh(jnp.sum(low_yx.astype(F32), 0))

    m_new = 0.9 * m_old.astype(F32) + 0.1 * low
    v_new = 0.999 * v_old.astype(F32) + 0.001 * low * low
    corr_one = 1.0 - 0.9**ADAM_STEP
    corr_two = 1.0 - 0.999**ADAM_STEP
    direction = (m_new / corr_one / (jnp.sqrt(v_new / corr_two) + 1e-08)).astype(BF16)

    rows = spread(direction, ("y", "x"), 16).reshape(640, 256)
    head_rows = head_matmul(scalar, grad_block, proj_weight, weight_other)
    rows, head_rows, mixed_out = lax.optimization_barrier((rows, head_rows, mixed_out))
    rows_other = lax.ppermute(rows, "core", CORE_SWAP)

    update = update_matmul(rows, rows_other, order, basis_own, basis_other)
    return (mixed_out, head_rows, update)


def solution(mesh):
    fine = Mesh(mesh.devices.reshape(SIZES), AXES)
    dp = ("y", "zh", "x")
    return jax.shard_map(
        shards,
        mesh=fine,
        in_specs=(
            P(dp + ("core",), "zl"),
            P("zl", "core"),
            P(dp + ("core", "zl"), None),
            P(dp, None),
            P("zl", dp, None),
            P("zl", dp, None),
        ),
        out_specs=(
            P(dp + ("core", "zl"), None),
            P(dp + ("core",), "zl"),
            P("zl", "core"),
        ),
        check_vma=False,
    )
```

```python
import jax
import jax.numpy as jnp
import numpy as np
from jax import lax
from jax.experimental import pallas as pl
from jax.experimental.pallas import tpu as pltpu
from jax.sharding import Mesh, PartitionSpec as P

ADAM_STEP = 10
BF16 = jnp.bfloat16
F32 = jnp.float32
AXES = ("y", "zh", "x", "core", "zl")
SIZES = (4, 4, 4, 2, 4)
CORE_SWAP = [(0, 1), (1, 0)]
PAIR = [(0, 1), (1, 0), (2, 3), (3, 2)]
MIRROR = [(0, 3), (3, 0), (1, 2), (2, 1)]
ORDER = np.eye(640, dtype=np.float32).reshape(640, 4, 4, 4, 10).transpose(0, 1, 3, 2, 4).reshape(640, 640)
ARRIVAL = np.eye(640, dtype=np.float32).reshape(640, 4, 4, 40).transpose(0, 2, 1, 3).reshape(640, 640)


def spread(values, axes, count):
    copies = jnp.broadcast_to(values[None], (count,) + values.shape)
    return lax.all_to_all(copies, axes, 0, 0, tiled=True)


def gather_zh(values):
    zh = lax.axis_index("zh")
    got = lax.ppermute(values, "zh", PAIR)
    odd = zh % 2 == 1
    pair = jnp.concatenate([jnp.where(odd, got, values), jnp.where(odd, values, got)], 0)
    got = lax.ppermute(pair, "zh", MIRROR)
    high = zh >= 2
    both = jnp.stack([jnp.where(high, got, pair), jnp.where(high, pair, got)])
    return both.reshape(4, *values.shape)


def sum_zh(values):
    for partners in (PAIR, MIRROR):
        sent = values.astype(BF16)
        values = sent.astype(F32) + lax.ppermute(sent, "zh", partners).astype(F32)
    return values


VMEM = pl.BlockSpec(memory_space=pltpu.VMEM)
SMEM = pl.BlockSpec(memory_space=pltpu.SMEM)
ROOM = pltpu.CompilerParams(vmem_limit_bytes=40 * 2**20)


def cost(flops, moved):
    return pl.CostEstimate(flops=flops, bytes_accessed=moved, transcendentals=0)


def columns_of(which, half):
    return pl.ds(pl.multiple_of(which * half, 128), half)


def mixed_kernel(core_ref, x_ref, own_ref, other_ref, out_ref):
    core = core_ref[0]
    half = own_ref.shape[1]
    for which, weight in ((core, own_ref), (1 - core, other_ref)):
        part = jnp.dot(x_ref[...], weight[...], preferred_element_type=F32)
        out_ref[:, columns_of(which, half)] = part.astype(BF16)


def mixed_matmul(core, x_heads, own, other):
    return pl.pallas_call(
        mixed_kernel,
        out_shape=jax.ShapeDtypeStruct((256, 2560), BF16),
        in_specs=[SMEM, VMEM, VMEM, VMEM],
        out_specs=VMEM,
        compiler_params=ROOM,
        cost_estimate=cost(2 * 256 * 640 * 2560, 5_000_000),
    )(core, x_heads, own, other)


def head_kernel(core_ref, grad_ref, own_ref, other_ref, out_ref):
    core = core_ref[0]
    half = own_ref.shape[1]
    total = None
    for which, weight in ((core, own_ref), (1 - core, other_ref)):
        part = lax.dot_general(
            grad_ref[:, columns_of(which, half)],
            weight[...],
            (((1,), (1,)), ((), ())),
            preferred_element_type=F32,
        )
        total = part if total is None else total + part
    out_ref[...] = total.astype(BF16)


def head_matmul(core, grads, own, other):
    return pl.pallas_call(
        head_kernel,
        out_shape=jax.ShapeDtypeStruct((256, 640), BF16),
        in_specs=[SMEM, VMEM, VMEM, VMEM],
        out_specs=VMEM,
        compiler_params=ROOM,
        cost_estimate=cost(2 * 256 * 640 * 2560, 5_000_000),
    )(core, grads, own, other)


def ordered_kernel(order_ref, arrival_ref, x_ref, xo_ref, g_ref, go_ref, px_ref, pxo_ref, pg_ref):
    for source, target in ((x_ref, px_ref), (xo_ref, pxo_ref)):
        moved = jnp.dot(source[...], order_ref[...], preferred_element_type=F32)
        target[...] = moved.astype(BF16)
    for which, source in ((0, g_ref), (1, go_ref)):
        for y in range(4):
            cols = slice(640 * y, 640 * (y + 1))
            moved = jnp.dot(source[:, cols], arrival_ref[...], preferred_element_type=F32)
            pg_ref[64 * which : 64 * (which + 1), cols] = moved.astype(BF16)


def ordered(order, arrival, rows, rows_other, grads, grads_other):
    x_shape = jax.ShapeDtypeStruct((256, 640), BF16)
    return pl.pallas_call(
        ordered_kernel,
        out_shape=(x_shape, x_shape, jax.ShapeDtypeStruct((128, 2560), BF16)),
        in_specs=[VMEM] * 6,
        out_specs=(VMEM,) * 3,
        compiler_params=ROOM,
        cost_estimate=cost(2 * 640 * 640 * 1024, 4_200_000),
    )(order, arrival, rows, rows_other, grads, grads_other)


def reduced_kernel(basis_ref, grad_ref, out_ref):
    part = jnp.dot(grad_ref[...], basis_ref[...], preferred_element_type=F32).astype(BF16)
    for target in range(out_ref.shape[0]):
        out_ref[target] = part


def reduced_matmul(basis, grads):
    return pl.pallas_call(
        reduced_kernel,
        out_shape=jax.ShapeDtypeStruct((4, 128, 256), BF16),
        in_specs=[VMEM] * 2,
        out_specs=VMEM,
        compiler_params=ROOM,
        cost_estimate=cost(2 * 128 * 256 * 2560, 2_500_000),
    )(basis, grads)


def low_kernel(reduced_ref, own_ref, other_ref, out_ref):
    total = None
    for which, rows in ((0, own_ref), (1, other_ref)):
        reduced = reduced_ref[:, 64 * which : 64 * (which + 1)].reshape(256, 256)
        part = lax.dot_general(
            rows[...], reduced, (((0,), (0,)), ((), ())), preferred_element_type=F32
        )
        total = part if total is None else total + part
    out_ref[...] = total.astype(BF16)


def low_matmul(reduced, rows, rows_other):
    return pl.pallas_call(
        low_kernel,
        out_shape=jax.ShapeDtypeStruct((640, 256), BF16),
        in_specs=[VMEM] * 3,
        out_specs=VMEM,
        compiler_params=ROOM,
        cost_estimate=cost(2 * 512 * 256 * 640, 1_500_000),
    )(reduced, rows, rows_other)


def update_kernel(own_ref, other_ref, order_ref, basis_ref, basis_other_ref, out_ref):
    total = None
    for rows, basis in ((own_ref, basis_ref), (other_ref, basis_other_ref)):
        direction = jnp.dot(order_ref[...], rows[...], preferred_element_type=F32).astype(BF16)
        part = lax.dot_general(
            direction, basis[...], (((1,), (1,)), ((), ())), preferred_element_type=F32
        )
        total = part if total is None else total + part
    out_ref[...] = total.astype(BF16)


def update_matmul(rows, rows_other, order, basis, basis_other):
    half = basis.shape[0]
    return pl.pallas_call(
        update_kernel,
        out_shape=jax.ShapeDtypeStruct((640, half), BF16),
        in_specs=[VMEM] * 5,
        out_specs=VMEM,
        compiler_params=ROOM,
        cost_estimate=cost(2 * 640 * 512 * (640 + half), 5_000_000),
    )(rows, rows_other, order, basis, basis_other)


def shards(x_heads, proj_weight, out_grad, proj_basis, first_moment, second_moment):
    core = lax.axis_index("core")
    half = proj_weight.shape[1]
    scalar = core.reshape(1).astype(jnp.int32)

    def own_columns(values):
        return lax.dynamic_slice_in_dim(values, core * 256, 256, 1)

    grad_block = lax.all_gather(out_grad, "zl", axis=0, tiled=True)
    weight_other = lax.ppermute(proj_weight, "core", CORE_SWAP)
    grad_other = lax.ppermute(out_grad, "core", CORE_SWAP)
    x_other = lax.ppermute(x_heads, "core", CORE_SWAP)

    parts = [proj_basis, first_moment[0].astype(BF16), second_moment[0].astype(BF16)]
    by_zh = gather_zh(jnp.concatenate([own_columns(part) for part in parts], 0))
    m_old = by_zh[:, 40:50].reshape(40, 256)
    v_old = by_zh[:, 50:].reshape(40, 256)
    by_yx = spread(by_zh[:, :40].reshape(160, 256), ("y", "x"), 16)

    mixed_part = mixed_matmul(scalar, x_heads, proj_weight, weight_other)
    order, arrival = jnp.asarray(ORDER, BF16), jnp.asarray(ARRIVAL, BF16)
    x_own, x_other, grads = ordered(order, arrival, x_heads, x_other, out_grad, grad_other)
    by_yx, mixed_part, x_own, x_other, grads, m_old, v_old = lax.optimization_barrier(
        (by_yx, mixed_part, x_own, x_other, grads, m_old, v_old)
    )

    mixed_out = lax.psum_scatter(mixed_part, "zl", scatter_dimension=0, tiled=True)

    reduced = reduced_matmul(by_yx.reshape(2560, 256), grads)
    reduced = lax.all_to_all(reduced, "zl", 0, 0, tiled=True)
    by_y = by_yx.reshape(2, 8, 160, 256)
    basis_own = lax.dynamic_index_in_dim(by_y, core, 0, keepdims=False)
    basis_other = lax.ppermute(
        lax.dynamic_index_in_dim(by_y, 1 - core, 0, keepdims=False), "core", CORE_SWAP
    )
    reduced, basis_other = lax.optimization_barrier((reduced, basis_other))

    low_chip = low_matmul(reduced, x_own, x_other)

    low_yx = lax.all_to_all(low_chip.reshape(16, 40, 256), ("y", "x"), 0, 0, tiled=True)
    basis_own, basis_other, low_chip = lax.optimization_barrier((basis_own, basis_other, low_chip))

    def natural(rows):
        return rows.reshape(2, 4, 4, 40, 256).transpose(0, 2, 1, 3, 4).reshape(half, 256)

    low_yx, basis_own, basis_other = lax.optimization_barrier(
        (low_yx, natural(basis_own), natural(basis_other))
    )
    low = sum_zh(jnp.sum(low_yx.astype(F32), 0))

    m_new = 0.9 * m_old.astype(F32) + 0.1 * low
    v_new = 0.999 * v_old.astype(F32) + 0.001 * low * low
    corr_one = 1.0 - 0.9**ADAM_STEP
    corr_two = 1.0 - 0.999**ADAM_STEP
    direction = (m_new / corr_one / (jnp.sqrt(v_new / corr_two) + 1e-08)).astype(BF16)

    rows = spread(direction, ("y", "x"), 16).reshape(640, 256)
    head_rows = head_matmul(scalar, grad_block, proj_weight, weight_other)
    rows, head_rows, mixed_out = lax.optimization_barrier((rows, head_rows, mixed_out))
    rows_other = lax.ppermute(rows, "core", CORE_SWAP)

    update = update_matmul(rows, rows_other, order, basis_own, basis_other)
    return (mixed_out, head_rows, update)


def solution(mesh):
    fine = Mesh(mesh.devices.reshape(SIZES), AXES)
    dp = ("y", "zh", "x")
    return jax.shard_map(
        shards,
        mesh=fine,
        in_specs=(
            P(dp + ("core",), "zl"),
            P("zl", "core"),
            P(dp + ("core", "zl"), None),
            P(dp, None),
            P("zl", dp, None),
            P("zl", dp, None),
        ),
        out_specs=(
            P(dp + ("core", "zl"), None),
            P(dp + ("core",), "zl"),
            P("zl", "core"),
        ),
        check_vma=False,
    )
```

```python
import jax
import jax.numpy as jnp
import numpy as np
from jax import lax
from jax.experimental import pallas as pl
from jax.experimental.pallas import tpu as pltpu
from jax.sharding import Mesh, PartitionSpec as P

ADAM_STEP = 10
BF16 = jnp.bfloat16
F32 = jnp.float32
AXES = ("y", "zh", "x", "core", "zl")
SIZES = (4, 4, 4, 2, 4)
CORE_SWAP = [(0, 1), (1, 0)]
PAIR = [(0, 1), (1, 0), (2, 3), (3, 2)]
MIRROR = [(0, 3), (3, 0), (1, 2), (2, 1)]
ORDER = np.eye(640, dtype=np.float32).reshape(640, 4, 4, 4, 10).transpose(0, 1, 3, 2, 4).reshape(640, 640)
ARRIVAL = np.eye(640, dtype=np.float32).reshape(640, 4, 4, 40).transpose(0, 2, 1, 3).reshape(640, 640)


def spread(values, axes, count):
    copies = jnp.broadcast_to(values[None], (count,) + values.shape)
    return lax.all_to_all(copies, axes, 0, 0, tiled=True)


def gather_zh(values):
    zh = lax.axis_index("zh")
    got = lax.ppermute(values, "zh", PAIR)
    odd = zh % 2 == 1
    pair = jnp.concatenate([jnp.where(odd, got, values), jnp.where(odd, values, got)], 0)
    got = lax.ppermute(pair, "zh", MIRROR)
    high = zh >= 2
    both = jnp.stack([jnp.where(high, got, pair), jnp.where(high, pair, got)])
    return both.reshape(4, *values.shape)


def sum_zh(values):
    for partners in (PAIR, MIRROR):
        sent = values.astype(BF16)
        values = sent.astype(F32) + lax.ppermute(sent, "zh", partners).astype(F32)
    return values


WHOLE = pl.BlockSpec()
SMEM = pl.BlockSpec(memory_space=pltpu.SMEM)
ROOM = pltpu.CompilerParams(vmem_limit_bytes=63 * 2**20)


def cost(flops, moved):
    return pl.CostEstimate(flops=flops, bytes_accessed=moved, transcendentals=0)


def columns_of(which, half):
    return pl.ds(pl.multiple_of(which * half, 128), half)


def mixed_kernel(core_ref, x_ref, own_ref, other_ref, out_ref):
    core = core_ref[0]
    half = own_ref.shape[1]
    for which, weight in ((core, own_ref), (1 - core, other_ref)):
        part = jnp.dot(x_ref[...], weight[...], preferred_element_type=F32)
        out_ref[:, columns_of(which, half)] = part.astype(BF16)


def mixed_matmul(core, x_heads, own, other):
    return pl.pallas_call(
        mixed_kernel,
        out_shape=jax.ShapeDtypeStruct((256, 2560), BF16),
        in_specs=[SMEM, WHOLE, WHOLE, WHOLE],
        out_specs=WHOLE,
        compiler_params=ROOM,
        cost_estimate=cost(2 * 256 * 640 * 2560, 5_000_000),
    )(core, x_heads, own, other)


def head_kernel(core_ref, grad_ref, own_ref, other_ref, out_ref):
    core = core_ref[0]
    half = own_ref.shape[1]
    total = None
    for which, weight in ((core, own_ref), (1 - core, other_ref)):
        part = lax.dot_general(
            grad_ref[:, columns_of(which, half)],
            weight[...],
            (((1,), (1,)), ((), ())),
            preferred_element_type=F32,
        )
        total = part if total is None else total + part
    out_ref[...] = total.astype(BF16)


def head_matmul(core, grads, own, other):
    return pl.pallas_call(
        head_kernel,
        out_shape=jax.ShapeDtypeStruct((256, 640), BF16),
        in_specs=[SMEM, WHOLE, WHOLE, WHOLE],
        out_specs=WHOLE,
        compiler_params=ROOM,
        cost_estimate=cost(2 * 256 * 640 * 2560, 5_000_000),
    )(core, grads, own, other)


def ordered_kernel(order_ref, arrival_ref, x_ref, xo_ref, g_ref, go_ref, px_ref, pxo_ref, pg_ref):
    for source, target in ((x_ref, px_ref), (xo_ref, pxo_ref)):
        moved = jnp.dot(source[...], order_ref[...], preferred_element_type=F32)
        target[...] = moved.astype(BF16)
    for which, source in ((0, g_ref), (1, go_ref)):
        for y in range(4):
            cols = slice(640 * y, 640 * (y + 1))
            moved = jnp.dot(source[:, cols], arrival_ref[...], preferred_element_type=F32)
            pg_ref[64 * which : 64 * (which + 1), cols] = moved.astype(BF16)


def ordered(order, arrival, rows, rows_other, grads, grads_other):
    x_shape = jax.ShapeDtypeStruct((256, 640), BF16)
    return pl.pallas_call(
        ordered_kernel,
        out_shape=(x_shape, x_shape, jax.ShapeDtypeStruct((128, 2560), BF16)),
        in_specs=[WHOLE] * 6,
        out_specs=(WHOLE,) * 3,
        compiler_params=ROOM,
        cost_estimate=cost(2 * 640 * 640 * 1024, 4_200_000),
    )(order, arrival, rows, rows_other, grads, grads_other)


def reduced_kernel(basis_ref, grad_ref, out_ref):
    part = jnp.dot(grad_ref[...], basis_ref[...], preferred_element_type=F32).astype(BF16)
    for target in range(out_ref.shape[0]):
        out_ref[target] = part


def reduced_matmul(basis, grads):
    return pl.pallas_call(
        reduced_kernel,
        out_shape=jax.ShapeDtypeStruct((4, 128, 256), BF16),
        in_specs=[WHOLE] * 2,
        out_specs=WHOLE,
        compiler_params=ROOM,
        cost_estimate=cost(2 * 128 * 256 * 2560, 2_500_000),
    )(basis, grads)


def low_kernel(reduced_ref, own_ref, other_ref, out_ref):
    total = None
    for which, rows in ((0, own_ref), (1, other_ref)):
        reduced = reduced_ref[:, 64 * which : 64 * (which + 1)].reshape(256, 256)
        part = lax.dot_general(
            rows[...], reduced, (((0,), (0,)), ((), ())), preferred_element_type=F32
        )
        total = part if total is None else total + part
    out_ref[...] = total.astype(BF16)


def low_matmul(reduced, rows, rows_other):
    return pl.pallas_call(
        low_kernel,
        out_shape=jax.ShapeDtypeStruct((640, 256), BF16),
        in_specs=[WHOLE] * 3,
        out_specs=WHOLE,
        compiler_params=ROOM,
        cost_estimate=cost(2 * 512 * 256 * 640, 1_500_000),
    )(reduced, rows, rows_other)


def update_kernel(own_ref, other_ref, order_ref, basis_ref, basis_other_ref, out_ref):
    total = None
    for rows, basis in ((own_ref, basis_ref), (other_ref, basis_other_ref)):
        direction = jnp.dot(order_ref[...], rows[...], preferred_element_type=F32).astype(BF16)
        part = lax.dot_general(
            direction, basis[...], (((1,), (1,)), ((), ())), preferred_element_type=F32
        )
        total = part if total is None else total + part
    out_ref[...] = total.astype(BF16)


def update_matmul(rows, rows_other, order, basis, basis_other):
    half = basis.shape[0]
    return pl.pallas_call(
        update_kernel,
        out_shape=jax.ShapeDtypeStruct((640, half), BF16),
        in_specs=[WHOLE] * 5,
        out_specs=WHOLE,
        compiler_params=ROOM,
        cost_estimate=cost(2 * 640 * 512 * (640 + half), 5_000_000),
    )(rows, rows_other, order, basis, basis_other)


def shards(x_heads, proj_weight, out_grad, proj_basis, first_moment, second_moment):
    core = lax.axis_index("core")
    half = proj_weight.shape[1]
    scalar = core.reshape(1).astype(jnp.int32)

    def own_columns(values):
        return lax.dynamic_slice_in_dim(values, core * 256, 256, 1)

    grad_block = lax.all_gather(out_grad, "zl", axis=0, tiled=True)
    weight_other = lax.ppermute(proj_weight, "core", CORE_SWAP)
    grad_other = lax.ppermute(out_grad, "core", CORE_SWAP)
    x_other = lax.ppermute(x_heads, "core", CORE_SWAP)

    parts = [proj_basis, first_moment[0].astype(BF16), second_moment[0].astype(BF16)]
    by_zh = gather_zh(jnp.concatenate([own_columns(part) for part in parts], 0))
    m_old = by_zh[:, 40:50].reshape(40, 256)
    v_old = by_zh[:, 50:].reshape(40, 256)
    by_yx = spread(by_zh[:, :40].reshape(160, 256), ("y", "x"), 16)

    mixed_part = mixed_matmul(scalar, x_heads, proj_weight, weight_other)
    order, arrival = jnp.asarray(ORDER, BF16), jnp.asarray(ARRIVAL, BF16)
    x_own, x_other, grads = ordered(order, arrival, x_heads, x_other, out_grad, grad_other)
    by_yx, mixed_part, x_own, x_other, grads, m_old, v_old = lax.optimization_barrier(
        (by_yx, mixed_part, x_own, x_other, grads, m_old, v_old)
    )

    mixed_out = lax.psum_scatter(mixed_part, "zl", scatter_dimension=0, tiled=True)

    reduced = reduced_matmul(by_yx.reshape(2560, 256), grads)
    reduced = lax.all_to_all(reduced, "zl", 0, 0, tiled=True)
    by_y = by_yx.reshape(2, 8, 160, 256)
    basis_own = lax.dynamic_index_in_dim(by_y, core, 0, keepdims=False)
    basis_other = lax.ppermute(
        lax.dynamic_index_in_dim(by_y, 1 - core, 0, keepdims=False), "core", CORE_SWAP
    )
    reduced, basis_other = lax.optimization_barrier((reduced, basis_other))

    low_chip = low_matmul(reduced, x_own, x_other)

    low_yx = lax.all_to_all(low_chip.reshape(16, 40, 256), ("y", "x"), 0, 0, tiled=True)
    basis_own, basis_other, low_chip = lax.optimization_barrier((basis_own, basis_other, low_chip))

    def natural(rows):
        return rows.reshape(2, 4, 4, 40, 256).transpose(0, 2, 1, 3, 4).reshape(half, 256)

    low_yx, basis_own, basis_other = lax.optimization_barrier(
        (low_yx, natural(basis_own), natural(basis_other))
    )
    low = sum_zh(jnp.sum(low_yx.astype(F32), 0))

    m_new = 0.9 * m_old.astype(F32) + 0.1 * low
    v_new = 0.999 * v_old.astype(F32) + 0.001 * low * low
    corr_one = 1.0 - 0.9**ADAM_STEP
    corr_two = 1.0 - 0.999**ADAM_STEP
    direction = (m_new / corr_one / (jnp.sqrt(v_new / corr_two) + 1e-08)).astype(BF16)

    rows = spread(direction, ("y", "x"), 16).reshape(640, 256)
    head_rows = head_matmul(scalar, grad_block, proj_weight, weight_other)
    rows, head_rows, mixed_out = lax.optimization_barrier((rows, head_rows, mixed_out))
    rows_other = lax.ppermute(rows, "core", CORE_SWAP)

    update = update_matmul(rows, rows_other, order, basis_own, basis_other)
    return (mixed_out, head_rows, update)


def solution(mesh):
    fine = Mesh(mesh.devices.reshape(SIZES), AXES)
    dp = ("y", "zh", "x")
    return jax.shard_map(
        shards,
        mesh=fine,
        in_specs=(
            P(dp + ("core",), "zl"),
            P("zl", "core"),
            P(dp + ("core", "zl"), None),
            P(dp, None),
            P("zl", dp, None),
            P("zl", dp, None),
        ),
        out_specs=(
            P(dp + ("core", "zl"), None),
            P(dp + ("core",), "zl"),
            P("zl", "core"),
        ),
        check_vma=False,
    )
```

```python
import jax
import jax.numpy as jnp
import numpy as np
from jax import lax
from jax.experimental import pallas as pl
from jax.experimental.pallas import tpu as pltpu
from jax.sharding import Mesh, PartitionSpec as P

ADAM_STEP = 10
BF16 = jnp.bfloat16
F32 = jnp.float32
AXES = ("y", "zh", "x", "core", "zl")
SIZES = (4, 4, 4, 2, 4)
CORE_SWAP = [(0, 1), (1, 0)]
PAIR = [(0, 1), (1, 0), (2, 3), (3, 2)]
MIRROR = [(0, 3), (3, 0), (1, 2), (2, 1)]
ORDER = np.eye(640, dtype=np.float32).reshape(640, 4, 4, 4, 10).transpose(0, 1, 3, 2, 4).reshape(640, 640)
ARRIVAL = np.eye(640, dtype=np.float32).reshape(640, 4, 4, 40).transpose(0, 2, 1, 3).reshape(640, 640)


def spread(values, axes, count):
    copies = jnp.broadcast_to(values[None], (count,) + values.shape)
    return lax.all_to_all(copies, axes, 0, 0, tiled=True)


def gather_zh(values):
    zh = lax.axis_index("zh")
    got = lax.ppermute(values, "zh", PAIR)
    odd = zh % 2 == 1
    pair = jnp.concatenate([jnp.where(odd, got, values), jnp.where(odd, values, got)], 0)
    got = lax.ppermute(pair, "zh", MIRROR)
    high = zh >= 2
    both = jnp.stack([jnp.where(high, got, pair), jnp.where(high, pair, got)])
    return both.reshape(4, *values.shape)


def sum_zh(values):
    for partners in (PAIR, MIRROR):
        sent = values.astype(BF16)
        values = sent.astype(F32) + lax.ppermute(sent, "zh", partners).astype(F32)
    return values


WHOLE = pl.BlockSpec()
FAR = pl.BlockSpec(memory_space=pltpu.HBM)
SMEM = pl.BlockSpec(memory_space=pltpu.SMEM)
ROOM = pltpu.CompilerParams(vmem_limit_bytes=63 * 2**20)


def cost(flops, moved):
    return pl.CostEstimate(flops=flops, bytes_accessed=moved, transcendentals=0)


def columns_of(which, half):
    return pl.ds(pl.multiple_of(which * half, 128), half)


def mixed_kernel(core_ref, x_ref, own_ref, other_ref, out_ref):
    core = core_ref[0]
    half = own_ref.shape[1]
    for which, weight in ((core, own_ref), (1 - core, other_ref)):
        part = jnp.dot(x_ref[...], weight[...], preferred_element_type=F32)
        out_ref[:, columns_of(which, half)] = part.astype(BF16)


def mixed_matmul(core, x_heads, own, other):
    return pl.pallas_call(
        mixed_kernel,
        out_shape=jax.ShapeDtypeStruct((256, 2560), BF16),
        in_specs=[SMEM, WHOLE, WHOLE, WHOLE],
        out_specs=WHOLE,
        compiler_params=ROOM,
        cost_estimate=cost(2 * 256 * 640 * 2560, 5_000_000),
    )(core, x_heads, own, other)


def head_kernel(core_ref, grad_ref, own_ref, other_ref, out_ref):
    core = core_ref[0]
    half = own_ref.shape[1]
    total = None
    for which, weight in ((core, own_ref), (1 - core, other_ref)):
        part = lax.dot_general(
            grad_ref[:, columns_of(which, half)],
            weight[...],
            (((1,), (1,)), ((), ())),
            preferred_element_type=F32,
        )
        total = part if total is None else total + part
    out_ref[...] = total.astype(BF16)


def head_matmul(core, grads, own, other):
    return pl.pallas_call(
        head_kernel,
        out_shape=jax.ShapeDtypeStruct((256, 640), BF16),
        in_specs=[SMEM, WHOLE, WHOLE, WHOLE],
        out_specs=WHOLE,
        compiler_params=ROOM,
        cost_estimate=cost(2 * 256 * 640 * 2560, 5_000_000),
    )(core, grads, own, other)


def ordered_kernel(order_ref, arrival_ref, x_ref, xo_ref, g_ref, go_ref, px_ref, pxo_ref, pg_ref):
    for source, target in ((x_ref, px_ref), (xo_ref, pxo_ref)):
        moved = jnp.dot(source[...], order_ref[...], preferred_element_type=F32)
        target[...] = moved.astype(BF16)
    for which, source in ((0, g_ref), (1, go_ref)):
        for y in range(4):
            cols = slice(640 * y, 640 * (y + 1))
            moved = jnp.dot(source[:, cols], arrival_ref[...], preferred_element_type=F32)
            pg_ref[64 * which : 64 * (which + 1), cols] = moved.astype(BF16)


def ordered(order, arrival, rows, rows_other, grads, grads_other):
    x_shape = jax.ShapeDtypeStruct((256, 640), BF16)
    return pl.pallas_call(
        ordered_kernel,
        out_shape=(x_shape, x_shape, jax.ShapeDtypeStruct((128, 2560), BF16)),
        in_specs=[WHOLE] * 6,
        out_specs=(WHOLE,) * 3,
        compiler_params=ROOM,
        cost_estimate=cost(2 * 640 * 640 * 1024, 4_200_000),
    )(order, arrival, rows, rows_other, grads, grads_other)


def fetch(pairs, sems):
    copies = [
        pltpu.make_async_copy(source, target, sems.at[i]) for i, (source, target) in enumerate(pairs)
    ]
    for copy in copies:
        copy.start()
    return copies


def reduced_kernel(basis_hbm, grad_hbm, out_ref, basis_ref, grad_ref, sems):
    blocks = [slice(640 * y, 640 * (y + 1)) for y in range(4)]
    pairs = [(grad_hbm, grad_ref)]
    pairs += [(basis_hbm.at[block], basis_ref.at[block]) for block in blocks]
    copies = fetch(pairs, sems)
    copies[0].wait()
    total = None
    for block, copy in zip(blocks, copies[1:]):
        copy.wait()
        part = jnp.dot(grad_ref[:, block], basis_ref[block], preferred_element_type=F32)
        total = part if total is None else total + part
    for target in range(out_ref.shape[0]):
        out_ref[target] = total.astype(BF16)


def reduced_matmul(basis, grads):
    return pl.pallas_call(
        reduced_kernel,
        out_shape=jax.ShapeDtypeStruct((4, 128, 256), BF16),
        in_specs=[FAR, FAR],
        out_specs=WHOLE,
        scratch_shapes=[
            pltpu.VMEM((2560, 256), BF16),
            pltpu.VMEM((128, 2560), BF16),
            pltpu.SemaphoreType.DMA((5,)),
        ],
        compiler_params=ROOM,
        cost_estimate=cost(2 * 128 * 256 * 2560, 2_500_000),
    )(basis, grads)


def low_kernel(reduced_hbm, own_hbm, other_hbm, out_ref, reduced_ref, rows_ref, sems):
    pairs = [(own_hbm, rows_ref.at[0]), (other_hbm, rows_ref.at[1]), (reduced_hbm, reduced_ref)]
    copies = fetch(pairs, sems)
    copies[2].wait()
    total = None
    for which in range(2):
        copies[which].wait()
        reduced = reduced_ref[:, 64 * which : 64 * (which + 1)].reshape(256, 256)
        part = lax.dot_general(
            rows_ref[which], reduced, (((0,), (0,)), ((), ())), preferred_element_type=F32
        )
        total = part if total is None else total + part
    out_ref[...] = total.astype(BF16)


def low_matmul(reduced, rows, rows_other):
    return pl.pallas_call(
        low_kernel,
        out_shape=jax.ShapeDtypeStruct((640, 256), BF16),
        in_specs=[FAR, FAR, FAR],
        out_specs=WHOLE,
        scratch_shapes=[
            pltpu.VMEM((4, 128, 256), BF16),
            pltpu.VMEM((2, 256, 640), BF16),
            pltpu.SemaphoreType.DMA((3,)),
        ],
        compiler_params=ROOM,
        cost_estimate=cost(2 * 512 * 256 * 640, 1_500_000),
    )(reduced, rows, rows_other)


def update_kernel(
    own_hbm, other_hbm, order_hbm, basis_hbm, basis_other_hbm, out_hbm,
    rows_ref, order_ref, basis_ref, out_ref, sems, out_sems,
):
    copies = fetch(
        [
            (order_hbm, order_ref),
            (own_hbm, rows_ref.at[0]),
            (other_hbm, rows_ref.at[1]),
            (basis_hbm, basis_ref.at[0]),
            (basis_other_hbm, basis_ref.at[1]),
        ],
        sems,
    )
    copies[0].wait()
    directions = []
    for which in range(2):
        copies[1 + which].wait()
        moved = jnp.dot(order_ref[...], rows_ref[which], preferred_element_type=F32)
        directions.append(moved.astype(BF16))
    copies[3].wait()
    copies[4].wait()
    leaving = []
    for block in range(out_ref.shape[0]):
        cols = slice(256 * block, 256 * (block + 1))
        parts = [
            lax.dot_general(
                directions[which],
                basis_ref[which, cols],
                (((1,), (1,)), ((), ())),
                preferred_element_type=F32,
            )
            for which in range(2)
        ]
        out_ref[block] = (parts[0] + parts[1]).astype(BF16)
        copy = pltpu.make_async_copy(out_ref.at[block], out_hbm.at[:, cols], out_sems.at[block])
        copy.start()
        leaving.append(copy)
    for copy in leaving:
        copy.wait()


def update_matmul(rows, rows_other, order, basis, basis_other):
    half = basis.shape[0]
    return pl.pallas_call(
        update_kernel,
        out_shape=jax.ShapeDtypeStruct((640, half), BF16),
        in_specs=[FAR] * 5,
        out_specs=FAR,
        scratch_shapes=[
            pltpu.VMEM((2, 640, 256), BF16),
            pltpu.VMEM((640, 640), BF16),
            pltpu.VMEM((2, half, 256), BF16),
            pltpu.VMEM((half // 256, 640, 256), BF16),
            pltpu.SemaphoreType.DMA((5,)),
            pltpu.SemaphoreType.DMA((half // 256,)),
        ],
        compiler_params=ROOM,
        cost_estimate=cost(2 * 640 * 512 * (640 + half), 5_000_000),
    )(rows, rows_other, order, basis, basis_other)


def shards(x_heads, proj_weight, out_grad, proj_basis, first_moment, second_moment):
    core = lax.axis_index("core")
    half = proj_weight.shape[1]
    scalar = core.reshape(1).astype(jnp.int32)

    def own_columns(values):
        return lax.dynamic_slice_in_dim(values, core * 256, 256, 1)

    grad_block = lax.all_gather(out_grad, "zl", axis=0, tiled=True)
    weight_other = lax.ppermute(proj_weight, "core", CORE_SWAP)
    grad_other = lax.ppermute(out_grad, "core", CORE_SWAP)
    x_other = lax.ppermute(x_heads, "core", CORE_SWAP)

    parts = [proj_basis, first_moment[0].astype(BF16), second_moment[0].astype(BF16)]
    by_zh = gather_zh(jnp.concatenate([own_columns(part) for part in parts], 0))
    m_old = by_zh[:, 40:50].reshape(40, 256)
    v_old = by_zh[:, 50:].reshape(40, 256)
    by_yx = spread(by_zh[:, :40].reshape(160, 256), ("y", "x"), 16)

    mixed_part = mixed_matmul(scalar, x_heads, proj_weight, weight_other)
    order, arrival = jnp.asarray(ORDER, BF16), jnp.asarray(ARRIVAL, BF16)
    x_own, x_other, grads = ordered(order, arrival, x_heads, x_other, out_grad, grad_other)
    by_yx, mixed_part, x_own, x_other, grads, m_old, v_old = lax.optimization_barrier(
        (by_yx, mixed_part, x_own, x_other, grads, m_old, v_old)
    )

    mixed_out = lax.psum_scatter(mixed_part, "zl", scatter_dimension=0, tiled=True)

    reduced = reduced_matmul(by_yx.reshape(2560, 256), grads)
    reduced = lax.all_to_all(reduced, "zl", 0, 0, tiled=True)
    by_y = by_yx.reshape(2, 8, 160, 256)
    basis_own = lax.dynamic_index_in_dim(by_y, core, 0, keepdims=False)
    basis_other = lax.ppermute(
        lax.dynamic_index_in_dim(by_y, 1 - core, 0, keepdims=False), "core", CORE_SWAP
    )
    reduced, basis_other = lax.optimization_barrier((reduced, basis_other))

    low_chip = low_matmul(reduced, x_own, x_other)

    low_yx = lax.all_to_all(low_chip.reshape(16, 40, 256), ("y", "x"), 0, 0, tiled=True)
    basis_own, basis_other, low_chip = lax.optimization_barrier((basis_own, basis_other, low_chip))

    def natural(rows):
        return rows.reshape(2, 4, 4, 40, 256).transpose(0, 2, 1, 3, 4).reshape(half, 256)

    low_yx, basis_own, basis_other = lax.optimization_barrier(
        (low_yx, natural(basis_own), natural(basis_other))
    )
    low = sum_zh(jnp.sum(low_yx.astype(F32), 0))

    m_new = 0.9 * m_old.astype(F32) + 0.1 * low
    v_new = 0.999 * v_old.astype(F32) + 0.001 * low * low
    corr_one = 1.0 - 0.9**ADAM_STEP
    corr_two = 1.0 - 0.999**ADAM_STEP
    direction = (m_new / corr_one / (jnp.sqrt(v_new / corr_two) + 1e-08)).astype(BF16)

    rows = spread(direction, ("y", "x"), 16).reshape(640, 256)
    head_rows = head_matmul(scalar, grad_block, proj_weight, weight_other)
    rows, head_rows, mixed_out = lax.optimization_barrier((rows, head_rows, mixed_out))
    rows_other = lax.ppermute(rows, "core", CORE_SWAP)

    update = update_matmul(rows, rows_other, order, basis_own, basis_other)
    return (mixed_out, head_rows, update)


def solution(mesh):
    fine = Mesh(mesh.devices.reshape(SIZES), AXES)
    dp = ("y", "zh", "x")
    return jax.shard_map(
        shards,
        mesh=fine,
        in_specs=(
            P(dp + ("core",), "zl"),
            P("zl", "core"),
            P(dp + ("core", "zl"), None),
            P(dp, None),
            P("zl", dp, None),
            P("zl", dp, None),
        ),
        out_specs=(
            P(dp + ("core", "zl"), None),
            P(dp + ("core",), "zl"),
            P("zl", "core"),
        ),
        check_vma=False,
    )
```

```python
import jax
import jax.numpy as jnp
import numpy as np
from jax import lax
from jax.experimental import pallas as pl
from jax.experimental.pallas import tpu as pltpu
from jax.sharding import Mesh, PartitionSpec as P

ADAM_STEP = 10
BF16 = jnp.bfloat16
F32 = jnp.float32
AXES = ("y", "zh", "x", "core", "zl")
SIZES = (4, 4, 4, 2, 4)
CORE_SWAP = [(0, 1), (1, 0)]
PAIR = [(0, 1), (1, 0), (2, 3), (3, 2)]
MIRROR = [(0, 3), (3, 0), (1, 2), (2, 1)]
ORDER = np.eye(640, dtype=np.float32).reshape(640, 4, 4, 4, 10).transpose(0, 1, 3, 2, 4).reshape(640, 640)


def spread(values, axes, count):
    copies = jnp.broadcast_to(values[None], (count,) + values.shape)
    return lax.all_to_all(copies, axes, 0, 0, tiled=True)


def gather_zh(values):
    zh = lax.axis_index("zh")
    got = lax.ppermute(values, "zh", PAIR)
    odd = zh % 2 == 1
    pair = jnp.concatenate([jnp.where(odd, got, values), jnp.where(odd, values, got)], 0)
    got = lax.ppermute(pair, "zh", MIRROR)
    high = zh >= 2
    both = jnp.stack([jnp.where(high, got, pair), jnp.where(high, pair, got)])
    return both.reshape(4, *values.shape)


def sum_zh(values):
    for partners in (PAIR, MIRROR):
        sent = values.astype(BF16)
        values = sent.astype(F32) + lax.ppermute(sent, "zh", partners).astype(F32)
    return values


VMEM = pl.BlockSpec(memory_space=pltpu.VMEM)
SMEM = pl.BlockSpec(memory_space=pltpu.SMEM)
ROOM = pltpu.CompilerParams(vmem_limit_bytes=40 * 2**20)


def cost(flops, moved):
    return pl.CostEstimate(flops=flops, bytes_accessed=moved, transcendentals=0)


def columns_of(which, half):
    return pl.ds(pl.multiple_of(which * half, 128), half)


def mixed_kernel(core_ref, x_ref, own_ref, other_ref, out_ref):
    core = core_ref[0]
    half = own_ref.shape[1]
    for which, weight in ((core, own_ref), (1 - core, other_ref)):
        part = jnp.dot(x_ref[...], weight[...], preferred_element_type=F32)
        out_ref[:, columns_of(which, half)] = part.astype(BF16)


def mixed_matmul(core, x_heads, own, other):
    return pl.pallas_call(
        mixed_kernel,
        out_shape=jax.ShapeDtypeStruct((256, 2560), BF16),
        in_specs=[SMEM, VMEM, VMEM, VMEM],
        out_specs=VMEM,
        compiler_params=ROOM,
        cost_estimate=cost(2 * 256 * 640 * 2560, 5_000_000),
    )(core, x_heads, own, other)


def head_kernel(core_ref, grad_ref, own_ref, other_ref, out_ref):
    core = core_ref[0]
    half = own_ref.shape[1]
    total = None
    for which, weight in ((core, own_ref), (1 - core, other_ref)):
        part = lax.dot_general(
            grad_ref[:, columns_of(which, half)],
            weight[...],
            (((1,), (1,)), ((), ())),
            preferred_element_type=F32,
        )
        total = part if total is None else total + part
    out_ref[...] = total.astype(BF16)


def head_matmul(core, grads, own, other):
    return pl.pallas_call(
        head_kernel,
        out_shape=jax.ShapeDtypeStruct((256, 640), BF16),
        in_specs=[SMEM, VMEM, VMEM, VMEM],
        out_specs=VMEM,
        compiler_params=ROOM,
        cost_estimate=cost(2 * 256 * 640 * 2560, 5_000_000),
    )(core, grads, own, other)


def ordered_kernel(order_ref, x_ref, xo_ref, px_ref, pxo_ref):
    for source, target in ((x_ref, px_ref), (xo_ref, pxo_ref)):
        moved = jnp.dot(source[...], order_ref[...], preferred_element_type=F32)
        target[...] = moved.astype(BF16)


def ordered(order, rows, rows_other):
    x_shape = jax.ShapeDtypeStruct((256, 640), BF16)
    whole = pl.BlockSpec()
    return pl.pallas_call(
        ordered_kernel,
        out_shape=(x_shape, x_shape),
        in_specs=[whole] * 3,
        out_specs=(whole,) * 2,
        compiler_params=pltpu.CompilerParams(vmem_limit_bytes=63 * 2**20),
        cost_estimate=cost(2 * 640 * 640 * 512, 2_200_000),
    )(order, rows, rows_other)


def low_kernel(basis_ref, x_ref, grad_ref, *refs):
    out_ref = refs[-1]
    reduced = jnp.dot(grad_ref[...], basis_ref[...], preferred_element_type=F32).astype(BF16)
    low = lax.dot_general(
        x_ref[...], reduced, (((0,), (0,)), ((), ())), preferred_element_type=F32
    )
    if len(refs) == 2:
        low = refs[0][...] + low
    out_ref[...] = low.astype(out_ref.dtype)


def low_matmul(basis, rows, grads, *before):
    return pl.pallas_call(
        low_kernel,
        out_shape=jax.ShapeDtypeStruct((640, 256), BF16 if before else F32),
        in_specs=[VMEM] * (3 + len(before)),
        out_specs=VMEM,
        compiler_params=ROOM,
        cost_estimate=cost(2 * 256 * 256 * (2560 + 640), 3_500_000),
    )(basis, rows, grads, *before)


def update_kernel(own_ref, other_ref, order_ref, basis_ref, basis_other_ref, out_ref):
    total = None
    for rows, basis in ((own_ref, basis_ref), (other_ref, basis_other_ref)):
        direction = jnp.dot(order_ref[...], rows[...], preferred_element_type=F32).astype(BF16)
        part = lax.dot_general(
            direction, basis[...], (((1,), (1,)), ((), ())), preferred_element_type=F32
        )
        total = part if total is None else total + part
    out_ref[...] = total.astype(BF16)


def update_matmul(rows, rows_other, order, basis, basis_other):
    half = basis.shape[0]
    return pl.pallas_call(
        update_kernel,
        out_shape=jax.ShapeDtypeStruct((640, half), BF16),
        in_specs=[VMEM] * 5,
        out_specs=VMEM,
        compiler_params=ROOM,
        cost_estimate=cost(2 * 640 * 512 * (640 + half), 5_000_000),
    )(rows, rows_other, order, basis, basis_other)


def shards(x_heads, proj_weight, out_grad, proj_basis, first_moment, second_moment):
    core = lax.axis_index("core")
    half = proj_weight.shape[1]
    scalar = core.reshape(1).astype(jnp.int32)

    def own_columns(values):
        return lax.dynamic_slice_in_dim(values, core * 256, 256, 1)

    grad_block = lax.all_gather(out_grad, "zl", axis=0, tiled=True)
    weight_other = lax.ppermute(proj_weight, "core", CORE_SWAP)
    x_other = lax.ppermute(x_heads, "core", CORE_SWAP)

    parts = [proj_basis, first_moment[0].astype(BF16), second_moment[0].astype(BF16)]
    by_zh = gather_zh(jnp.concatenate([own_columns(part) for part in parts], 0))
    m_old = by_zh[:, 40:50].reshape(40, 256)
    v_old = by_zh[:, 50:].reshape(40, 256)
    by_yx = spread(by_zh[:, :40].reshape(160, 256), ("y", "x"), 16)

    mixed_part = mixed_matmul(scalar, x_heads, proj_weight, weight_other)
    order = jnp.asarray(ORDER, BF16)
    x_own, x_other = ordered(order, x_heads, x_other)
    by_yx, mixed_part, x_own, x_other, m_old, v_old = lax.optimization_barrier(
        (by_yx, mixed_part, x_own, x_other, m_old, v_old)
    )
    basis_cols = by_yx.reshape(4, 4, 4, 40, 256).transpose(0, 2, 1, 3, 4).reshape(2560, 256)

    mixed_out = lax.psum_scatter(mixed_part, "zl", scatter_dimension=0, tiled=True)

    basis_own = lax.dynamic_slice_in_dim(basis_cols, core * half, half, 0)
    basis_sent = lax.dynamic_slice_in_dim(basis_cols, (1 - core) * half, half, 0)
    basis_cols, basis_own, basis_sent, grad_block = lax.optimization_barrier(
        (basis_cols, basis_own, basis_sent, grad_block)
    )
    basis_other = lax.ppermute(basis_sent, "core", CORE_SWAP)

    grad_other = lax.ppermute(grad_block, "core", CORE_SWAP)
    low_own = low_matmul(basis_cols, x_own, grad_block)
    low_own, basis_other = lax.optimization_barrier((low_own, basis_other))
    low_chip = low_matmul(basis_cols, x_other, grad_other, low_own)

    low_yx = lax.all_to_all(low_chip.reshape(16, 40, 256), ("y", "x"), 0, 0, tiled=True)
    low = sum_zh(jnp.sum(low_yx.astype(F32), 0))

    m_new = 0.9 * m_old.astype(F32) + 0.1 * low
    v_new = 0.999 * v_old.astype(F32) + 0.001 * low * low
    corr_one = 1.0 - 0.9**ADAM_STEP
    corr_two = 1.0 - 0.999**ADAM_STEP
    direction = (m_new / corr_one / (jnp.sqrt(v_new / corr_two) + 1e-08)).astype(BF16)

    rows = spread(direction, ("y", "x"), 16).reshape(640, 256)
    head_rows = head_matmul(scalar, grad_block, proj_weight, weight_other)
    rows, head_rows, mixed_out = lax.optimization_barrier((rows, head_rows, mixed_out))
    rows_other = lax.ppermute(rows, "core", CORE_SWAP)

    update = update_matmul(rows, rows_other, order, basis_own, basis_other)
    return (mixed_out, head_rows, update)


def solution(mesh):
    fine = Mesh(mesh.devices.reshape(SIZES), AXES)
    dp = ("y", "zh", "x")
    return jax.shard_map(
        shards,
        mesh=fine,
        in_specs=(
            P(dp + ("core",), "zl"),
            P("zl", "core"),
            P(dp + ("core", "zl"), None),
            P(dp, None),
            P("zl", dp, None),
            P("zl", dp, None),
        ),
        out_specs=(
            P(dp + ("core", "zl"), None),
            P(dp + ("core",), "zl"),
            P("zl", "core"),
        ),
        check_vma=False,
    )
```

```python
import jax
import jax.numpy as jnp
import numpy as np
from jax import lax
from jax.experimental import pallas as pl
from jax.experimental.pallas import tpu as pltpu
from jax.sharding import Mesh, PartitionSpec as P

ADAM_STEP = 10
BF16 = jnp.bfloat16
F32 = jnp.float32
AXES = ("y", "zh", "x", "core", "zl")
SIZES = (4, 4, 4, 2, 4)
CORE_SWAP = [(0, 1), (1, 0)]
PAIR = [(0, 1), (1, 0), (2, 3), (3, 2)]
MIRROR = [(0, 3), (3, 0), (1, 2), (2, 1)]
ORDER = np.eye(640, dtype=np.float32).reshape(640, 4, 4, 4, 10).transpose(0, 1, 3, 2, 4).reshape(640, 640)


def spread(values, axes, count):
    copies = jnp.broadcast_to(values[None], (count,) + values.shape)
    return lax.all_to_all(copies, axes, 0, 0, tiled=True)


def gather_zh(values):
    zh = lax.axis_index("zh")
    got = lax.ppermute(values, "zh", PAIR)
    odd = zh % 2 == 1
    pair = jnp.concatenate([jnp.where(odd, got, values), jnp.where(odd, values, got)], 0)
    got = lax.ppermute(pair, "zh", MIRROR)
    high = zh >= 2
    both = jnp.stack([jnp.where(high, got, pair), jnp.where(high, pair, got)])
    return both.reshape(4, *values.shape)


def sum_zh(values):
    for partners in (PAIR, MIRROR):
        sent = values.astype(BF16)
        values = sent.astype(F32) + lax.ppermute(sent, "zh", partners).astype(F32)
    return values


VMEM = pl.BlockSpec(memory_space=pltpu.VMEM)
SMEM = pl.BlockSpec(memory_space=pltpu.SMEM)
FAR = pl.BlockSpec(memory_space=pltpu.HBM)
ROOM = pltpu.CompilerParams(vmem_limit_bytes=40 * 2**20)
ALL = pltpu.CompilerParams(vmem_limit_bytes=63 * 2**20)


def cost(flops, moved):
    return pl.CostEstimate(flops=flops, bytes_accessed=moved, transcendentals=0)


def columns_of(which, half):
    return pl.ds(pl.multiple_of(which * half, 128), half)


def mixed_kernel(core_ref, x_ref, own_ref, other_ref, out_ref):
    core = core_ref[0]
    half = own_ref.shape[1]
    for which, weight in ((core, own_ref), (1 - core, other_ref)):
        part = jnp.dot(x_ref[...], weight[...], preferred_element_type=F32)
        out_ref[:, columns_of(which, half)] = part.astype(BF16)


def mixed_matmul(core, x_heads, own, other):
    return pl.pallas_call(
        mixed_kernel,
        out_shape=jax.ShapeDtypeStruct((256, 2560), BF16),
        in_specs=[SMEM, VMEM, VMEM, VMEM],
        out_specs=VMEM,
        compiler_params=ROOM,
        cost_estimate=cost(2 * 256 * 640 * 2560, 5_000_000),
    )(core, x_heads, own, other)


def head_kernel(core_ref, grad_ref, own_ref, other_ref, out_ref):
    core = core_ref[0]
    half = own_ref.shape[1]
    total = None
    for which, weight in ((core, own_ref), (1 - core, other_ref)):
        part = lax.dot_general(
            grad_ref[:, columns_of(which, half)],
            weight[...],
            (((1,), (1,)), ((), ())),
            preferred_element_type=F32,
        )
        total = part if total is None else total + part
    out_ref[...] = total.astype(BF16)


def head_matmul(core, grads, own, other):
    return pl.pallas_call(
        head_kernel,
        out_shape=jax.ShapeDtypeStruct((256, 640), BF16),
        in_specs=[SMEM, VMEM, VMEM, VMEM],
        out_specs=VMEM,
        compiler_params=ROOM,
        cost_estimate=cost(2 * 256 * 640 * 2560, 5_000_000),
    )(core, grads, own, other)


def ordered_kernel(order_ref, x_ref, xo_ref, px_ref, pxo_ref):
    for source, target in ((x_ref, px_ref), (xo_ref, pxo_ref)):
        moved = jnp.dot(source[...], order_ref[...], preferred_element_type=F32)
        target[...] = moved.astype(BF16)


def ordered(order, rows, rows_other):
    x_shape = jax.ShapeDtypeStruct((256, 640), BF16)
    whole = pl.BlockSpec()
    return pl.pallas_call(
        ordered_kernel,
        out_shape=(x_shape, x_shape),
        in_specs=[whole] * 3,
        out_specs=(whole,) * 2,
        compiler_params=ALL,
        cost_estimate=cost(2 * 640 * 640 * 512, 2_200_000),
    )(order, rows, rows_other)


def low_kernel(basis_ref, x_ref, grad_ref, *refs):
    out_ref = refs[-1]
    reduced = jnp.dot(grad_ref[...], basis_ref[...], preferred_element_type=F32).astype(BF16)
    low = lax.dot_general(
        x_ref[...], reduced, (((0,), (0,)), ((), ())), preferred_element_type=F32
    )
    if len(refs) == 2:
        low = refs[0][...] + low
    out_ref[...] = low.astype(out_ref.dtype)


def low_matmul(basis, rows, grads, *before):
    return pl.pallas_call(
        low_kernel,
        out_shape=jax.ShapeDtypeStruct((640, 256), BF16 if before else F32),
        in_specs=[VMEM] * (3 + len(before)),
        out_specs=VMEM,
        compiler_params=ROOM,
        cost_estimate=cost(2 * 256 * 256 * (2560 + 640), 3_500_000),
    )(basis, rows, grads, *before)


def fetch(pairs, sems):
    copies = [
        pltpu.make_async_copy(source, target, sems.at[i]) for i, (source, target) in enumerate(pairs)
    ]
    for copy in copies:
        copy.start()
    return copies


def update_kernel(
    place_ref, own_hbm, other_hbm, basis_hbm, basis_other_hbm, out_hbm,
    rows_ref, basis_ref, out_ref, sems, out_sems,
):
    copies = fetch(
        [
            (own_hbm, rows_ref.at[0]),
            (other_hbm, rows_ref.at[1]),
            (basis_hbm, basis_ref.at[0]),
            (basis_other_hbm, basis_ref.at[1]),
        ],
        sems,
    )
    natural = lax.broadcasted_iota(jnp.int32, (640, 640), 0)
    order = jnp.where(natural == place_ref[...], 1.0, 0.0).astype(BF16)
    directions = []
    for which in range(2):
        copies[which].wait()
        moved = jnp.dot(order, rows_ref[which], preferred_element_type=F32)
        directions.append(moved.astype(BF16))
    copies[2].wait()
    copies[3].wait()
    leaving = []
    for block in range(out_ref.shape[0]):
        cols = slice(256 * block, 256 * (block + 1))
        parts = [
            lax.dot_general(
                directions[which],
                basis_ref[which, cols],
                (((1,), (1,)), ((), ())),
                preferred_element_type=F32,
            )
            for which in range(2)
        ]
        out_ref[block] = (parts[0] + parts[1]).astype(BF16)
        copy = pltpu.make_async_copy(out_ref.at[block], out_hbm.at[:, cols], out_sems.at[block])
        copy.start()
        leaving.append(copy)
    for copy in leaving:
        copy.wait()


def update_matmul(place, rows, rows_other, basis, basis_other):
    half = basis.shape[0]
    return pl.pallas_call(
        update_kernel,
        out_shape=jax.ShapeDtypeStruct((640, half), BF16),
        in_specs=[pl.BlockSpec()] + [FAR] * 4,
        out_specs=FAR,
        scratch_shapes=[
            pltpu.VMEM((2, 640, 256), BF16),
            pltpu.VMEM((2, half, 256), BF16),
            pltpu.VMEM((half // 256, 640, 256), BF16),
            pltpu.SemaphoreType.DMA((4,)),
            pltpu.SemaphoreType.DMA((half // 256,)),
        ],
        compiler_params=ALL,
        cost_estimate=cost(2 * 640 * 512 * (640 + half), 5_000_000),
    )(place, rows, rows_other, basis, basis_other)


def shards(x_heads, proj_weight, out_grad, proj_basis, first_moment, second_moment):
    core = lax.axis_index("core")
    half = proj_weight.shape[1]
    scalar = core.reshape(1).astype(jnp.int32)

    def own_columns(values):
        return lax.dynamic_slice_in_dim(values, core * 256, 256, 1)

    grad_block = lax.all_gather(out_grad, "zl", axis=0, tiled=True)
    weight_other = lax.ppermute(proj_weight, "core", CORE_SWAP)
    x_other = lax.ppermute(x_heads, "core", CORE_SWAP)

    parts = [proj_basis, first_moment[0].astype(BF16), second_moment[0].astype(BF16)]
    by_zh = gather_zh(jnp.concatenate([own_columns(part) for part in parts], 0))
    m_old = by_zh[:, 40:50].reshape(40, 256)
    v_old = by_zh[:, 50:].reshape(40, 256)
    by_yx = spread(by_zh[:, :40].reshape(160, 256), ("y", "x"), 16)

    mixed_part = mixed_matmul(scalar, x_heads, proj_weight, weight_other)
    order = jnp.asarray(ORDER, BF16)
    x_own, x_other = ordered(order, x_heads, x_other)
    by_yx, mixed_part, x_own, x_other, m_old, v_old = lax.optimization_barrier(
        (by_yx, mixed_part, x_own, x_other, m_old, v_old)
    )
    basis_cols = by_yx.reshape(4, 4, 4, 40, 256).transpose(0, 2, 1, 3, 4).reshape(2560, 256)

    mixed_out = lax.psum_scatter(mixed_part, "zl", scatter_dimension=0, tiled=True)

    basis_own = lax.dynamic_slice_in_dim(basis_cols, core * half, half, 0)
    basis_sent = lax.dynamic_slice_in_dim(basis_cols, (1 - core) * half, half, 0)
    basis_cols, basis_own, basis_sent, grad_block = lax.optimization_barrier(
        (basis_cols, basis_own, basis_sent, grad_block)
    )
    basis_other = lax.ppermute(basis_sent, "core", CORE_SWAP)

    grad_other = lax.ppermute(grad_block, "core", CORE_SWAP)
    low_own = low_matmul(basis_cols, x_own, grad_block)
    low_own, basis_other = lax.optimization_barrier((low_own, basis_other))
    low_chip = low_matmul(basis_cols, x_other, grad_other, low_own)

    low_yx = lax.all_to_all(low_chip.reshape(16, 40, 256), ("y", "x"), 0, 0, tiled=True)
    low = sum_zh(jnp.sum(low_yx.astype(F32), 0))

    m_new = 0.9 * m_old.astype(F32) + 0.1 * low
    v_new = 0.999 * v_old.astype(F32) + 0.001 * low * low
    corr_one = 1.0 - 0.9**ADAM_STEP
    corr_two = 1.0 - 0.999**ADAM_STEP
    direction = (m_new / corr_one / (jnp.sqrt(v_new / corr_two) + 1e-08)).astype(BF16)

    rows = spread(direction, ("y", "x"), 16).reshape(640, 256)
    head_rows = head_matmul(scalar, grad_block, proj_weight, weight_other)
    rows, head_rows, mixed_out = lax.optimization_barrier((rows, head_rows, mixed_out))
    rows_other = lax.ppermute(rows, "core", CORE_SWAP)

    place = jnp.asarray(ORDER.argmax(0).reshape(1, 640), jnp.int32)
    update = update_matmul(place, rows, rows_other, basis_own, basis_other)
    return (mixed_out, head_rows, update)


def solution(mesh):
    fine = Mesh(mesh.devices.reshape(SIZES), AXES)
    dp = ("y", "zh", "x")
    return jax.shard_map(
        shards,
        mesh=fine,
        in_specs=(
            P(dp + ("core",), "zl"),
            P("zl", "core"),
            P(dp + ("core", "zl"), None),
            P(dp, None),
            P("zl", dp, None),
            P("zl", dp, None),
        ),
        out_specs=(
            P(dp + ("core", "zl"), None),
            P(dp + ("core",), "zl"),
            P("zl", "core"),
        ),
        check_vma=False,
    )
```

```python
import jax
import jax.numpy as jnp
import numpy as np
from jax import lax
from jax.experimental import pallas as pl
from jax.experimental.pallas import tpu as pltpu
from jax.sharding import Mesh, PartitionSpec as P

ADAM_STEP = 10
BF16 = jnp.bfloat16
F32 = jnp.float32
AXES = ("y", "zh", "x", "core", "zl")
SIZES = (4, 4, 4, 2, 4)
CORE_SWAP = [(0, 1), (1, 0)]
PAIR = [(0, 1), (1, 0), (2, 3), (3, 2)]
MIRROR = [(0, 3), (3, 0), (1, 2), (2, 1)]
ORDER = np.eye(640, dtype=np.float32).reshape(640, 4, 4, 4, 10).transpose(0, 1, 3, 2, 4).reshape(640, 640)


def spread(values, axes, count):
    copies = jnp.broadcast_to(values[None], (count,) + values.shape)
    return lax.all_to_all(copies, axes, 0, 0, tiled=True)


def gather_zh(values):
    zh = lax.axis_index("zh")
    got = lax.ppermute(values, "zh", PAIR)
    odd = zh % 2 == 1
    pair = jnp.concatenate([jnp.where(odd, got, values), jnp.where(odd, values, got)], 0)
    got = lax.ppermute(pair, "zh", MIRROR)
    high = zh >= 2
    both = jnp.stack([jnp.where(high, got, pair), jnp.where(high, pair, got)])
    return both.reshape(4, *values.shape)


def sum_zh(values):
    for partners in (PAIR, MIRROR):
        sent = values.astype(BF16)
        values = sent.astype(F32) + lax.ppermute(sent, "zh", partners).astype(F32)
    return values


VMEM = pl.BlockSpec(memory_space=pltpu.VMEM)
SMEM = pl.BlockSpec(memory_space=pltpu.SMEM)
ROOM = pltpu.CompilerParams(vmem_limit_bytes=40 * 2**20)


def cost(flops, moved):
    return pl.CostEstimate(flops=flops, bytes_accessed=moved, transcendentals=0)


def columns_of(which, half):
    return pl.ds(pl.multiple_of(which * half, 128), half)


def mixed_kernel(core_ref, x_ref, own_ref, other_ref, out_ref):
    core = core_ref[0]
    half = own_ref.shape[1]
    for which, weight in ((core, own_ref), (1 - core, other_ref)):
        part = jnp.dot(x_ref[...], weight[...], preferred_element_type=F32)
        out_ref[:, columns_of(which, half)] = part.astype(BF16)


def mixed_matmul(core, x_heads, own, other):
    return pl.pallas_call(
        mixed_kernel,
        out_shape=jax.ShapeDtypeStruct((256, 2560), BF16),
        in_specs=[SMEM, VMEM, VMEM, VMEM],
        out_specs=VMEM,
        compiler_params=ROOM,
        cost_estimate=cost(2 * 256 * 640 * 2560, 5_000_000),
    )(core, x_heads, own, other)


def head_kernel(core_ref, grad_ref, own_ref, other_ref, out_ref):
    core = core_ref[0]
    half = own_ref.shape[1]
    total = None
    for which, weight in ((core, own_ref), (1 - core, other_ref)):
        part = lax.dot_general(
            grad_ref[:, columns_of(which, half)],
            weight[...],
            (((1,), (1,)), ((), ())),
            preferred_element_type=F32,
        )
        total = part if total is None else total + part
    out_ref[...] = total.astype(BF16)


def head_matmul(core, grads, own, other):
    return pl.pallas_call(
        head_kernel,
        out_shape=jax.ShapeDtypeStruct((256, 640), BF16),
        in_specs=[SMEM, VMEM, VMEM, VMEM],
        out_specs=VMEM,
        compiler_params=ROOM,
        cost_estimate=cost(2 * 256 * 640 * 2560, 5_000_000),
    )(core, grads, own, other)


def ordered_kernel(order_ref, x_ref, xo_ref, px_ref, pxo_ref):
    for source, target in ((x_ref, px_ref), (xo_ref, pxo_ref)):
        moved = jnp.dot(source[...], order_ref[...], preferred_element_type=F32)
        target[...] = moved.astype(BF16)


def ordered(order, rows, rows_other):
    x_shape = jax.ShapeDtypeStruct((256, 640), BF16)
    whole = pl.BlockSpec()
    return pl.pallas_call(
        ordered_kernel,
        out_shape=(x_shape, x_shape),
        in_specs=[whole] * 3,
        out_specs=(whole,) * 2,
        compiler_params=pltpu.CompilerParams(vmem_limit_bytes=63 * 2**20),
        cost_estimate=cost(2 * 640 * 640 * 512, 2_200_000),
    )(order, rows, rows_other)


def low_kernel(basis_ref, x_ref, grad_ref, *refs):
    out_ref = refs[-1]
    reduced = jnp.dot(grad_ref[...], basis_ref[...], preferred_element_type=F32).astype(BF16)
    low = lax.dot_general(
        x_ref[...], reduced, (((0,), (0,)), ((), ())), preferred_element_type=F32
    )
    if len(refs) == 2:
        low = refs[0][...] + low
    out_ref[...] = low.astype(out_ref.dtype)


def low_matmul(basis, rows, grads, *before):
    return pl.pallas_call(
        low_kernel,
        out_shape=jax.ShapeDtypeStruct((640, 256), BF16 if before else F32),
        in_specs=[VMEM] * (3 + len(before)),
        out_specs=VMEM,
        compiler_params=ROOM,
        cost_estimate=cost(2 * 256 * 256 * (2560 + 640), 3_500_000),
    )(basis, rows, grads, *before)


def update_kernel(core_ref, rows_ref, order_ref, basis_ref, basis_other_ref, out_ref):
    core = core_ref[0]
    total = None
    for which, basis in ((core, basis_ref), (1 - core, basis_other_ref)):
        direction = jnp.dot(
            order_ref[...], rows_ref[which], preferred_element_type=F32
        ).astype(BF16)
        part = lax.dot_general(
            direction, basis[...], (((1,), (1,)), ((), ())), preferred_element_type=F32
        )
        total = part if total is None else total + part
    out_ref[...] = total.astype(BF16)


def update_matmul(core, rows, order, basis, basis_other):
    half = basis.shape[0]
    return pl.pallas_call(
        update_kernel,
        out_shape=jax.ShapeDtypeStruct((640, half), BF16),
        in_specs=[SMEM] + [VMEM] * 4,
        out_specs=VMEM,
        compiler_params=ROOM,
        cost_estimate=cost(2 * 640 * 512 * (640 + half), 5_000_000),
    )(core, rows, order, basis, basis_other)


def shards(x_heads, proj_weight, out_grad, proj_basis, first_moment, second_moment):
    core = lax.axis_index("core")
    half = proj_weight.shape[1]
    scalar = core.reshape(1).astype(jnp.int32)

    def own_columns(values):
        return lax.dynamic_slice_in_dim(values, core * 256, 256, 1)

    grad_block = lax.all_gather(out_grad, "zl", axis=0, tiled=True)
    weight_other = lax.ppermute(proj_weight, "core", CORE_SWAP)
    x_other = lax.ppermute(x_heads, "core", CORE_SWAP)

    parts = [proj_basis, first_moment[0].astype(BF16), second_moment[0].astype(BF16)]
    by_zh = gather_zh(jnp.concatenate([own_columns(part) for part in parts], 0))
    m_old = by_zh[:, 40:50].reshape(40, 256)
    v_old = by_zh[:, 50:].reshape(40, 256)
    by_yx = spread(by_zh[:, :40].reshape(160, 256), ("y", "x"), 16)

    mixed_part = mixed_matmul(scalar, x_heads, proj_weight, weight_other)
    order = jnp.asarray(ORDER, BF16)
    x_own, x_other = ordered(order, x_heads, x_other)
    by_yx, mixed_part, x_own, x_other, m_old, v_old = lax.optimization_barrier(
        (by_yx, mixed_part, x_own, x_other, m_old, v_old)
    )
    basis_cols = by_yx.reshape(4, 4, 4, 40, 256).transpose(0, 2, 1, 3, 4).reshape(2560, 256)

    mixed_out = lax.psum_scatter(mixed_part, "zl", scatter_dimension=0, tiled=True)

    basis_own = lax.dynamic_slice_in_dim(basis_cols, core * half, half, 0)
    basis_sent = lax.dynamic_slice_in_dim(basis_cols, (1 - core) * half, half, 0)
    basis_cols, basis_own, basis_sent, grad_block = lax.optimization_barrier(
        (basis_cols, basis_own, basis_sent, grad_block)
    )
    basis_other = lax.ppermute(basis_sent, "core", CORE_SWAP)

    grad_other = lax.ppermute(grad_block, "core", CORE_SWAP)
    low_own = low_matmul(basis_cols, x_own, grad_block)
    low_own, basis_other = lax.optimization_barrier((low_own, basis_other))
    low_chip = low_matmul(basis_cols, x_other, grad_other, low_own)

    low_yx = lax.all_to_all(low_chip.reshape(16, 40, 256), ("y", "x"), 0, 0, tiled=True)
    low = sum_zh(jnp.sum(low_yx.astype(F32), 0))

    m_new = 0.9 * m_old.astype(F32) + 0.1 * low
    v_new = 0.999 * v_old.astype(F32) + 0.001 * low * low
    corr_one = 1.0 - 0.9**ADAM_STEP
    corr_two = 1.0 - 0.999**ADAM_STEP
    direction = (m_new / corr_one / (jnp.sqrt(v_new / corr_two) + 1e-08)).astype(BF16)

    rows = spread(direction, ("core", "y", "x"), 32).reshape(2, 640, 256)
    head_rows = head_matmul(scalar, grad_block, proj_weight, weight_other)
    rows, head_rows, mixed_out = lax.optimization_barrier((rows, head_rows, mixed_out))

    update = update_matmul(scalar, rows, order, basis_own, basis_other)
    return (mixed_out, head_rows, update)


def solution(mesh):
    fine = Mesh(mesh.devices.reshape(SIZES), AXES)
    dp = ("y", "zh", "x")
    return jax.shard_map(
        shards,
        mesh=fine,
        in_specs=(
            P(dp + ("core",), "zl"),
            P("zl", "core"),
            P(dp + ("core", "zl"), None),
            P(dp, None),
            P("zl", dp, None),
            P("zl", dp, None),
        ),
        out_specs=(
            P(dp + ("core", "zl"), None),
            P(dp + ("core",), "zl"),
            P("zl", "core"),
        ),
        check_vma=False,
    )
```

```python
import jax
import jax.numpy as jnp
import numpy as np
from jax import lax
from jax.experimental import pallas as pl
from jax.experimental.pallas import tpu as pltpu
from jax.sharding import Mesh, PartitionSpec as P

ADAM_STEP = 10
BF16 = jnp.bfloat16
F32 = jnp.float32
AXES = ("y", "zh", "x", "core", "zl")
SIZES = (4, 4, 4, 2, 4)
CORE_SWAP = [(0, 1), (1, 0)]
PAIR = [(0, 1), (1, 0), (2, 3), (3, 2)]
MIRROR = [(0, 3), (3, 0), (1, 2), (2, 1)]
ORDER = np.eye(640, dtype=np.float32).reshape(640, 4, 4, 4, 10).transpose(0, 1, 3, 2, 4).reshape(640, 640)


def spread(values, axes, count):
    copies = jnp.broadcast_to(values[None], (count,) + values.shape)
    return lax.all_to_all(copies, axes, 0, 0, tiled=True)


def gather_zh(values):
    zh = lax.axis_index("zh")
    got = lax.ppermute(values, "zh", PAIR)
    odd = zh % 2 == 1
    pair = jnp.concatenate([jnp.where(odd, got, values), jnp.where(odd, values, got)], 0)
    got = lax.ppermute(pair, "zh", MIRROR)
    high = zh >= 2
    both = jnp.stack([jnp.where(high, got, pair), jnp.where(high, pair, got)])
    return both.reshape(4, *values.shape)


def sum_zh(values):
    for partners in (PAIR, MIRROR):
        sent = values.astype(BF16)
        values = sent.astype(F32) + lax.ppermute(sent, "zh", partners).astype(F32)
    return values


VMEM = pl.BlockSpec(memory_space=pltpu.VMEM)
SMEM = pl.BlockSpec(memory_space=pltpu.SMEM)
FAR = pl.BlockSpec(memory_space=pltpu.HBM)
ROOM = pltpu.CompilerParams(vmem_limit_bytes=40 * 2**20)
ALL = pltpu.CompilerParams(vmem_limit_bytes=63 * 2**20)


def cost(flops, moved):
    return pl.CostEstimate(flops=flops, bytes_accessed=moved, transcendentals=0)


def columns_of(which, half):
    return pl.ds(pl.multiple_of(which * half, 128), half)


def mixed_kernel(core_ref, x_ref, own_ref, other_ref, out_ref):
    core = core_ref[0]
    half = own_ref.shape[1]
    for which, weight in ((core, own_ref), (1 - core, other_ref)):
        part = jnp.dot(x_ref[...], weight[...], preferred_element_type=F32)
        out_ref[:, columns_of(which, half)] = part.astype(BF16)


def mixed_matmul(core, x_heads, own, other):
    return pl.pallas_call(
        mixed_kernel,
        out_shape=jax.ShapeDtypeStruct((256, 2560), BF16),
        in_specs=[SMEM, VMEM, VMEM, VMEM],
        out_specs=VMEM,
        compiler_params=ROOM,
        cost_estimate=cost(2 * 256 * 640 * 2560, 5_000_000),
    )(core, x_heads, own, other)


def head_kernel(core_ref, grad_ref, own_ref, other_ref, out_ref):
    core = core_ref[0]
    half = own_ref.shape[1]
    total = None
    for which, weight in ((core, own_ref), (1 - core, other_ref)):
        part = lax.dot_general(
            grad_ref[:, columns_of(which, half)],
            weight[...],
            (((1,), (1,)), ((), ())),
            preferred_element_type=F32,
        )
        total = part if total is None else total + part
    out_ref[...] = total.astype(BF16)


def head_matmul(core, grads, own, other):
    return pl.pallas_call(
        head_kernel,
        out_shape=jax.ShapeDtypeStruct((256, 640), BF16),
        in_specs=[SMEM, VMEM, VMEM, VMEM],
        out_specs=VMEM,
        compiler_params=ROOM,
        cost_estimate=cost(2 * 256 * 640 * 2560, 5_000_000),
    )(core, grads, own, other)


def ordered_kernel(order_ref, x_ref, xo_ref, px_ref, pxo_ref):
    for source, target in ((x_ref, px_ref), (xo_ref, pxo_ref)):
        moved = jnp.dot(source[...], order_ref[...], preferred_element_type=F32)
        target[...] = moved.astype(BF16)


def ordered(order, rows, rows_other):
    x_shape = jax.ShapeDtypeStruct((256, 640), BF16)
    whole = pl.BlockSpec()
    return pl.pallas_call(
        ordered_kernel,
        out_shape=(x_shape, x_shape),
        in_specs=[whole] * 3,
        out_specs=(whole,) * 2,
        compiler_params=ALL,
        cost_estimate=cost(2 * 640 * 640 * 512, 2_200_000),
    )(order, rows, rows_other)


def low_kernel(basis_ref, x_ref, grad_ref, *refs):
    out_ref = refs[-1]
    reduced = jnp.dot(grad_ref[...], basis_ref[...], preferred_element_type=F32).astype(BF16)
    low = lax.dot_general(
        x_ref[...], reduced, (((0,), (0,)), ((), ())), preferred_element_type=F32
    )
    if len(refs) == 2:
        low = refs[0][...] + low
    out_ref[...] = low.astype(out_ref.dtype)


def low_matmul(basis, rows, grads, *before):
    return pl.pallas_call(
        low_kernel,
        out_shape=jax.ShapeDtypeStruct((640, 256), BF16 if before else F32),
        in_specs=[VMEM] * (3 + len(before)),
        out_specs=VMEM,
        compiler_params=ROOM,
        cost_estimate=cost(2 * 256 * 256 * (2560 + 640), 3_500_000),
    )(basis, rows, grads, *before)


def fetch(pairs, sems):
    copies = [
        pltpu.make_async_copy(source, target, sems.at[i]) for i, (source, target) in enumerate(pairs)
    ]
    for copy in copies:
        copy.start()
    return copies


def update_kernel(
    own_hbm, other_hbm, order_hbm, basis_hbm, basis_other_hbm, out_hbm,
    rows_ref, order_ref, basis_ref, out_ref, sems, out_sems,
):
    copies = fetch(
        [
            (order_hbm, order_ref),
            (own_hbm, rows_ref.at[0]),
            (other_hbm, rows_ref.at[1]),
            (basis_hbm, basis_ref.at[0]),
            (basis_other_hbm, basis_ref.at[1]),
        ],
        sems,
    )
    copies[0].wait()
    directions = []
    for which in range(2):
        copies[1 + which].wait()
        moved = jnp.dot(order_ref[...], rows_ref[which], preferred_element_type=F32)
        directions.append(moved.astype(BF16))
    copies[3].wait()
    copies[4].wait()
    leaving = []
    for block in range(out_ref.shape[0]):
        cols = slice(256 * block, 256 * (block + 1))
        parts = [
            lax.dot_general(
                directions[which],
                basis_ref[which, cols],
                (((1,), (1,)), ((), ())),
                preferred_element_type=F32,
            )
            for which in range(2)
        ]
        out_ref[block] = (parts[0] + parts[1]).astype(BF16)
        copy = pltpu.make_async_copy(out_ref.at[block], out_hbm.at[:, cols], out_sems.at[block])
        copy.start()
        leaving.append(copy)
    for copy in leaving:
        copy.wait()


def update_matmul(rows, rows_other, order, basis, basis_other):
    half = basis.shape[0]
    return pl.pallas_call(
        update_kernel,
        out_shape=jax.ShapeDtypeStruct((640, half), BF16),
        in_specs=[FAR] * 5,
        out_specs=FAR,
        scratch_shapes=[
            pltpu.VMEM((2, 640, 256), BF16),
            pltpu.VMEM((640, 640), BF16),
            pltpu.VMEM((2, half, 256), BF16),
            pltpu.VMEM((half // 256, 640, 256), BF16),
            pltpu.SemaphoreType.DMA((5,)),
            pltpu.SemaphoreType.DMA((half // 256,)),
        ],
        compiler_params=ALL,
        cost_estimate=cost(2 * 640 * 512 * (640 + half), 5_000_000),
    )(rows, rows_other, order, basis, basis_other)


def shards(x_heads, proj_weight, out_grad, proj_basis, first_moment, second_moment):
    core = lax.axis_index("core")
    half = proj_weight.shape[1]
    scalar = core.reshape(1).astype(jnp.int32)

    def own_columns(values):
        return lax.dynamic_slice_in_dim(values, core * 256, 256, 1)

    grad_block = lax.all_gather(out_grad, "zl", axis=0, tiled=True)
    weight_other = lax.ppermute(proj_weight, "core", CORE_SWAP)
    x_other = lax.ppermute(x_heads, "core", CORE_SWAP)

    parts = [proj_basis, first_moment[0].astype(BF16), second_moment[0].astype(BF16)]
    by_zh = gather_zh(jnp.concatenate([own_columns(part) for part in parts], 0))
    m_old = by_zh[:, 40:50].reshape(40, 256)
    v_old = by_zh[:, 50:].reshape(40, 256)
    by_yx = spread(by_zh[:, :40].reshape(160, 256), ("y", "x"), 16)

    mixed_part = mixed_matmul(scalar, x_heads, proj_weight, weight_other)
    order = jnp.asarray(ORDER, BF16)
    x_own, x_other = ordered(order, x_heads, x_other)
    by_yx, mixed_part, x_own, x_other, m_old, v_old = lax.optimization_barrier(
        (by_yx, mixed_part, x_own, x_other, m_old, v_old)
    )
    basis_cols = by_yx.reshape(4, 4, 4, 40, 256).transpose(0, 2, 1, 3, 4).reshape(2560, 256)

    mixed_out = lax.psum_scatter(mixed_part, "zl", scatter_dimension=0, tiled=True)

    basis_own = lax.dynamic_slice_in_dim(basis_cols, core * half, half, 0)
    basis_sent = lax.dynamic_slice_in_dim(basis_cols, (1 - core) * half, half, 0)
    basis_cols, basis_own, basis_sent, grad_block = lax.optimization_barrier(
        (basis_cols, basis_own, basis_sent, grad_block)
    )
    basis_other = lax.ppermute(basis_sent, "core", CORE_SWAP)

    grad_other = lax.ppermute(grad_block, "core", CORE_SWAP)
    low_own = low_matmul(basis_cols, x_own, grad_block)
    low_own, basis_other = lax.optimization_barrier((low_own, basis_other))
    low_chip = low_matmul(basis_cols, x_other, grad_other, low_own)

    low_yx = lax.all_to_all(low_chip.reshape(16, 40, 256), ("y", "x"), 0, 0, tiled=True)
    low = sum_zh(jnp.sum(low_yx.astype(F32), 0))

    m_new = 0.9 * m_old.astype(F32) + 0.1 * low
    v_new = 0.999 * v_old.astype(F32) + 0.001 * low * low
    corr_one = 1.0 - 0.9**ADAM_STEP
    corr_two = 1.0 - 0.999**ADAM_STEP
    direction = (m_new / corr_one / (jnp.sqrt(v_new / corr_two) + 1e-08)).astype(BF16)

    rows = spread(direction, ("y", "x"), 16).reshape(640, 256)
    head_rows = head_matmul(scalar, grad_block, proj_weight, weight_other)
    rows, head_rows, mixed_out = lax.optimization_barrier((rows, head_rows, mixed_out))
    rows_other = lax.ppermute(rows, "core", CORE_SWAP)

    update = update_matmul(rows, rows_other, order, basis_own, basis_other)
    return (mixed_out, head_rows, update)


def solution(mesh):
    fine = Mesh(mesh.devices.reshape(SIZES), AXES)
    dp = ("y", "zh", "x")
    return jax.shard_map(
        shards,
        mesh=fine,
        in_specs=(
            P(dp + ("core",), "zl"),
            P("zl", "core"),
            P(dp + ("core", "zl"), None),
            P(dp, None),
            P("zl", dp, None),
            P("zl", dp, None),
        ),
        out_specs=(
            P(dp + ("core", "zl"), None),
            P(dp + ("core",), "zl"),
            P("zl", "core"),
        ),
        check_vma=False,
    )
```
